32 devices in a mesh: gx: 4 (over y, x), gy: 2 (over core), gz: 4 (over z).
Axes of the slice: x: 2, y: 2, z: 4, core: 2. Of those that a mesh axis runs over, the one named last changes fastest.
Arguments:
- fine: float32 [5, 64, 32, 512], P(None, 'gx', 'gy', 'gz'), as said below
- shell: float32 [4, 64, 3840], P('gx', ('gy', 'gz')), as said below
- parent: int32 [4, 64], P('gx'), may hold values from 0 to 63, as said below
- link: int32 [6, 4, 2, 32], P(None, 'gx', 'gy', 'gz'), may hold values 0 or 1
Outputs:
- fine_new: float32 [5, 64, 32, 512], P(None, 'gx', 'gy', 'gz')
- coarse_new: float32 [4, 64, 2560], P('gx', ('gy', 'gz'))
The draws below stay inside these ranges and needn't reach their ends.
Inputs may be any that keep to these rules, and one draw needn't show every extreme that they name: Each row parent[i, :] names every slot 0 to 63 exactly once. Of the 8 blocks q = d * 8 to d * 8 + 7 of a row, at most 2 have parents among the slots o * 8 to o * 8 + 7 of any one o, and every such pair that meets at all holds exactly 2. `fine`: density and energy make pressure positive in every cell; velocities stay well below the sound speed times a few. `shell`: same physical ranges as fine.
All inputs are finite; a program needn't handle non-finite values. No bound on the sum of `link` on one device may be relied on, other than what follows from the above.
Results may differ from the reference program's by a relative error of at most 0.0003.
Values sent between devices are 32-bit elements; how exact they have to be, the bound alone decides.
A program may use at most 128 MiB of HBM per device.

```python
import jax
import jax.numpy as jnp
from jax import lax

BS = 16
BLK = 8
CAP = 2
NBZ = 32
NQ = 64
NX = 64
NY = 32
NZ = 512
SHELL = 3840
COARSE = 2560
N_GX = 4
N_GY = 2
N_GZ = 4


def conserved(key, shape):
    keys = jax.random.split(key, 5)
    rho = jnp.exp(jax.random.uniform(keys[0], shape, jnp.float32, jnp.log(0.5), jnp.log(2.0)))
    press = jnp.exp(jax.random.uniform(keys[1], shape, jnp.float32, jnp.log(0.5), jnp.log(2.0)))
    vels = [0.5 * jnp.clip(jax.random.normal(keys[2 + c], shape, jnp.float32), -3.0, 3.0) for c in range(3)]
    kinetic = 0.5 * rho * (vels[0] * vels[0] + vels[1] * vels[1] + vels[2] * vels[2])
    energy = press / 0.4 + kinetic
    return [rho, rho * vels[0], rho * vels[1], rho * vels[2], energy]


def draw_fine(key, part):
    fields = conserved(jax.random.fold_in(key, 11), (NX, NY, NZ))
    return jnp.stack(fields, axis=0).astype(jnp.float32)


def draw_shell(key, part):
    half = BS // 2
    fields = conserved(jax.random.fold_in(key, 23), (N_GX, NQ, 2, 6, half * half))
    stacked = jnp.stack(fields, axis=4)
    return stacked.reshape(N_GX, NQ, SHELL).astype(jnp.float32)


def draw_parent(key, part):
    groups = N_GY * N_GZ
    base = jax.random.fold_in(key, 37)
    result = []
    for row in range(N_GX):
        row_key = jax.random.fold_in(base, row)
        order = jax.random.permutation(jax.random.fold_in(row_key, 1), groups).astype(jnp.int32)
        slot_keys = jax.random.split(jax.random.fold_in(row_key, 2), groups)
        shuffles = jax.vmap(lambda one: jax.random.permutation(one, BLK).astype(jnp.int32))(slot_keys)
        device = jnp.arange(groups, dtype=jnp.int32)[:, None]
        local = jnp.arange(BLK, dtype=jnp.int32)[None, :]
        group = local // CAP
        owner = (order[device] + group) % groups
        within = group * CAP + local % CAP
        placed = shuffles[owner, within]
        result.append((owner * BLK + placed).reshape(NQ))
    return jnp.stack(result, axis=0).astype(jnp.int32)


def with_ends(drawn, own_key, least, high):
    index_at = [jax.random.randint(jax.random.fold_in(own_key, axis), (), 0, length) for axis, length in enumerate(drawn.shape)]
    widest = drawn.shape.index(max(drawn.shape))
    beside = index_at[:widest] + [(index_at[widest] + 1) % drawn.shape[widest]] + index_at[widest + 1:]
    return drawn.at[tuple(index_at)].set(least).at[tuple(beside)].set(high)


def setup_inputs(seed: int = 0) -> dict:
    streams_of = jax.random.split(jax.random.key(seed), 5)
    return {
        "fine": draw_fine(jax.random.fold_in(streams_of[4], 71), 0),
        "shell": draw_shell(jax.random.fold_in(streams_of[4], 71), 0),
        "parent": draw_parent(jax.random.fold_in(streams_of[4], 71), 0),
        "link": with_ends((jax.random.randint(streams_of[3], (6, N_GX, N_GY, NBZ), 0, 3) < 2).astype(jnp.int32), jax.random.fold_in(streams_of[3], 1), 0, 1),
    }


GAMMA = 1.4
LAMBDA = 0.05

def flux_terms(ext, direc):
    rho = ext[:, 0]
    mom = ext[:, 1:4]
    energy = ext[:, 4]
    vel = mom / rho[:, None]
    press = (GAMMA - 1.0) * (energy - 0.5 * lax.optimization_barrier(jnp.sum(mom * vel, axis=1)))
    normal = vel[:, direc]
    parts = [mom[:, direc], mom[:, 0] * normal, mom[:, 1] * normal, mom[:, 2] * normal, (energy + press) * normal]
    parts[1 + direc] = parts[1 + direc] + press
    flux = jnp.stack(parts, axis=1)
    speed = jnp.abs(normal) + jnp.sqrt(GAMMA * press / rho)
    return (flux, speed)

def interface(ext, direc):
    flux, speed = flux_terms(ext, direc)
    dim = 2 + direc
    count = ext.shape[dim]
    f_left = lax.slice_in_dim(flux, 0, count - 1, axis=dim)
    f_right = lax.slice_in_dim(flux, 1, count, axis=dim)
    u_left = lax.slice_in_dim(ext, 0, count - 1, axis=dim)
    u_right = lax.slice_in_dim(ext, 1, count, axis=dim)
    wave = jnp.maximum(lax.slice_in_dim(speed, 0, count - 1, axis=dim - 1), lax.slice_in_dim(speed, 1, count, axis=dim - 1))
    face = 0.5 * (f_left + f_right) - 0.5 * wave[:, None] * (u_right - u_left)
    return lax.slice_in_dim(face, 1, count - 1, axis=dim) - lax.slice_in_dim(face, 0, count - 2, axis=dim)

def advance(core, ghosts):
    ext_x = jnp.concatenate([ghosts[0][:, :, None], core, ghosts[1][:, :, None]], axis=2)
    ext_y = jnp.concatenate([ghosts[2][:, :, :, None], core, ghosts[3][:, :, :, None]], axis=3)
    ext_z = jnp.concatenate([ghosts[4][..., None], core, ghosts[5][..., None]], axis=4)
    total = interface(ext_x, 0) + interface(ext_y, 1) + interface(ext_z, 2)
    return core - LAMBDA * total

def inject(coarse):
    return jnp.repeat(jnp.repeat(coarse, 2, axis=-2), 2, axis=-1)

def mix_ghosts(fine_faces, coarse_faces, links):
    result = []
    for face in range(6):
        chosen = links[:, face][:, None, None, None] == 1
        result.append(jnp.where(chosen, fine_faces[face], inject(coarse_faces[:, face])))
    return result

def restrict(core):
    count = core.shape[0]
    half = core.shape[2] // 2
    grouped = core.reshape(count, 5, half, 2, half, 2, half, 2)
    return grouped.mean(axis=(3, 5, 7)).reshape(count, -1)

def reference(fine, shell, parent, link):
    half = BS // 2
    blocks = fine.reshape(5, N_GX, BS, N_GY, BS, NBZ, BS).transpose(1, 3, 5, 0, 2, 4, 6)
    fetched = jnp.take_along_axis(shell, parent[:, :, None], axis=1)
    fetched = fetched.reshape(N_GX, N_GY, NBZ, 2, 6, 5, half, half)
    level_now = fetched[:, :, :, 0]
    level_mid = 0.5 * (fetched[:, :, :, 0] + fetched[:, :, :, 1])
    links = link.transpose(1, 2, 3, 0)
    rows = N_GX * N_GY
    for step in range(2):
        level = level_now if step == 0 else level_mid
        faces = [jnp.roll(blocks[:, :, :, :, BS - 1], 1, axis=0), jnp.roll(blocks[:, :, :, :, 0], -1, axis=0), jnp.roll(blocks[:, :, :, :, :, BS - 1], 1, axis=1), jnp.roll(blocks[:, :, :, :, :, 0], -1, axis=1), jnp.roll(blocks[..., BS - 1], 1, axis=2), jnp.roll(blocks[..., 0], -1, axis=2)]

        def update(items):
            core, fx0, fx1, fy0, fy1, fz0, fz1, level_row, link_row = items
            ghosts = mix_ghosts([fx0, fx1, fy0, fy1, fz0, fz1], level_row, link_row)
            return advance(core, ghosts)
        packed = tuple((a.reshape((rows, NBZ) + a.shape[3:]) for a in [blocks] + faces + [level, links]))
        blocks = lax.map(update, packed).reshape(blocks.shape)
    restricted = lax.map(restrict, blocks.reshape((rows, NBZ) + blocks.shape[3:]))
    restricted = restricted.reshape(N_GX, NQ, COARSE)
    inverse = jnp.argsort(parent, axis=1).astype(jnp.int32)
    coarse_new = jnp.take_along_axis(restricted, inverse[:, :, None], axis=1)
    fine_new = blocks.transpose(3, 0, 4, 1, 5, 2, 6).reshape(5, NX, NY, NZ)
    return (fine_new, coarse_new)
```

```python
import functools

import jax
import jax.numpy as jnp
from jax import lax
from jax.experimental import pallas as pl
from jax.experimental.pallas import tpu as pltpu
from jax.sharding import PartitionSpec as P

BS = 16
GAMMA = 1.4
LAMBDA = 0.05
LANES = 128
MESH = pl.DeviceIdType.MESH
F32 = jnp.float32
BF16 = jnp.bfloat16


def iota(shape, dim):
    return lax.broadcasted_iota(jnp.int32, shape, dim)


def parts_of(x, count):
    result = []
    for _ in range(count - 1):
        head = x.astype(BF16).astype(F32)
        result.append(head)
        x = x - head
    result.append(x)
    return result


def dot(a, b, contract):
    return lax.dot_general(a, b, (contract, ((), ())), preferred_element_type=F32)


def stacked(x):
    pieces = parts_of(x, 3)
    if x.shape[0] % 16:
        pieces.append(jnp.zeros_like(x))
    return jnp.concatenate(pieces, axis=0).astype(BF16)


def beside(x, rows):
    count = 4 if rows % 16 else 3
    return jnp.concatenate([x] * count, axis=1).astype(BF16)


def prim(u):
    inv = 1.0 / u[0]
    vel = [u[1] * inv, u[2] * inv, u[3] * inv]
    press = (GAMMA - 1.0) * (u[4] - 0.5 * (u[1] * vel[0] + u[2] * vel[1] + u[3] * vel[2]))
    sound = jnp.sqrt(GAMMA * press * inv)
    return vel, press, sound


def flux(u, pr, d):
    vel, press, sound = pr
    vd = vel[d]
    f = [u[1 + d], u[1] * vd, u[2] * vd, u[3] * vd, (u[4] + press) * vd]
    f[1 + d] = f[1 + d] + press
    return f, jnp.abs(vd) + sound


def interface(ul, fl, sl, ur, fr, sr, sign=0.5):
    wave = sign * jnp.maximum(sl, sr)
    return [0.5 * (fl[i] + fr[i]) - wave * (ur[i] - ul[i]) for i in range(5)]


def kernel(
    n,
    fine, shell, parent, link, out, coarse,
    s0, s1, ypack, zpack, hx, hy, hz, sstage, srecv, rstage, rrecv, xt, cxy, cz, hyf, xy, zt,
    load_sem, halo_send, halo_recv, all_send, all_recv,
):
    nx, ny, nz = n
    group = ny * nz
    count = 2 * group
    gx, gy, gz = lax.axis_index("gx"), lax.axis_index("gy"), lax.axis_index("gz")
    me = gy * nz + gz
    blk = shell.shape[1]
    width = shell.shape[2] // 2
    chunks = width // LANES
    rwidth = coarse.shape[2]
    rchunks = rwidth // LANES
    nq = parent.shape[1]
    peers = []
    for i in range(1, group):
        peer = lax.rem(me + i, group)
        peers.append((gx, peer // nz, lax.rem(peer, nz)))
    xlo, xhi = (lax.rem(gx + nx - 1, nx), gy, gz), (lax.rem(gx + 1, nx), gy, gz)
    ylo, yhi = (gx, lax.rem(gy + ny - 1, ny), gz), (gx, lax.rem(gy + 1, ny), gz)
    zlo, zhi = (gx, gy, lax.rem(gz + nz - 1, nz)), (gx, gy, lax.rem(gz + 1, nz))

    barrier = pltpu.get_barrier_semaphore()
    greeted = peers + [xlo, xhi]
    for dev in greeted:
        pl.semaphore_signal(barrier, inc=1, device_id=dev, device_id_type=MESH)

    loads = []
    for f in range(5):
        load = pltpu.make_async_copy(fine.at[f], s0.at[f, pl.ds(BS, BS * BS)], load_sem.at[f])
        load.start()
        loads.append(load)

    par = parent[...]
    lane_q = iota((1, nq), 1)
    owner = par // blk
    rank = jnp.zeros((1, nq), jnp.int32)
    for j in range(1, blk):
        before = pltpu.roll(jnp.broadcast_to(owner, (8, nq)), j, 1)[0:1]
        rank = rank + jnp.where((lane_q % blk >= j) & (before == owner), 1, 0)
    at_owner = (lane_q // blk) * 2 + rank
    at_block = owner * 2 + rank
    to_t = (jnp.broadcast_to(at_owner, (count, nq)) == iota((count, nq), 0)).astype(F32).astype(BF16)
    mine = (jnp.broadcast_to(par, (blk, nq)) == me * blk + iota((blk, nq), 0)).astype(F32).astype(BF16)
    sel_ts = dot(to_t, mine, ((1,), (1,)))
    sel_st = dot(mine, to_t, ((1,), (1,)))
    at_block8 = jnp.broadcast_to(at_block.astype(F32), (8, nq)).astype(BF16)
    spread = (iota((nq, LANES), 0) == me * blk + iota((nq, LANES), 1) // BS).astype(F32).astype(BF16)
    pick = (iota((nq, blk), 0) == me * blk + iota((nq, blk), 1)).astype(F32).astype(BF16)
    row_lane = dot(at_block8, spread, ((1,), (0,)))[0:1]
    row_blk = dot(at_block8, pick, ((1,), (0,)))[0:1]
    be = (jnp.broadcast_to(row_lane, (count, LANES)) == iota((count, LANES), 0).astype(F32)).astype(F32)
    be3 = jnp.concatenate([be] * 3, axis=0).astype(BF16)
    sel_tk = (jnp.broadcast_to(row_blk, (count, blk)) == iota((count, blk), 0).astype(F32)).astype(F32)

    sel = beside(sel_ts, blk)
    for c in range(chunks):
        now = shell[0, :, pl.ds(c * LANES, LANES)]
        end = shell[0, :, pl.ds(width + c * LANES, LANES)]
        both = jnp.concatenate([stacked(now), stacked(0.5 * (now + end))], axis=1)
        rows = dot(sel, both, ((1,), (0,)))
        sstage[0, pl.ds(c, count, stride=16), :] = rows[:, :LANES]
        sstage[1, pl.ds(c, count, stride=16), :] = rows[:, LANES:]

    lane = iota((BS, LANES), 1)
    sub = iota((BS, LANES), 0)

    def plane(ref, f, x):
        return ref[f, pl.ds(pl.multiple_of((x + 1) * BS, BS), BS), :]

    def pack_y(ref):
        for f in range(5):
            ypack[0, f] = ref[f, pl.ds(BS, BS, stride=BS), :]
            ypack[1, f] = ref[f, pl.ds(2 * BS - 1, BS, stride=BS), :]

    def pack_z(ref):
        def body(x, acc):
            a0, a1 = acc
            for f in range(4):
                i = f * BS + x
                a0 = jnp.where(lane // 2 == i, pltpu.roll(plane(ref, f, x), 2 * i + 1, 1), a0)
            a1 = jnp.where(lane // 2 == x, pltpu.roll(plane(ref, 4, x), 2 * x + 1, 1), a1)
            return a0, a1

        zero = jnp.zeros((BS, LANES), F32)
        a0, a1 = lax.fori_loop(0, BS, body, (zero, zero))
        zpack[0] = a0
        zpack[1] = a1

    def halos(ref, step):
        def send(k, src, dst, dev):
            copy = pltpu.make_async_remote_copy(
                src_ref=src, dst_ref=dst, send_sem=halo_send.at[step, k], recv_sem=halo_recv.at[step, k],
                device_id=dev, device_id_type=MESH,
            )
            copy.start()
            return copy

        return [
            send(0, ref.at[:, pl.ds(BS * BS, BS)], hx.at[step, 0], xhi),
            send(1, ref.at[:, pl.ds(BS, BS)], hx.at[step, 1], xlo),
            send(2, ypack.at[1], hy.at[step, 0], yhi),
            send(3, ypack.at[0], hy.at[step, 1], ylo),
            send(4, zpack, hz.at[step, 0], zhi),
            send(5, zpack, hz.at[step, 1], zlo),
        ]

    def exchange(kind, stage, recv, rows):
        copies = []
        for i, dev in enumerate(peers):
            to = lax.rem(me + i + 1, group)
            copy = pltpu.make_async_remote_copy(
                src_ref=stage.at[pl.ds(pl.multiple_of(to * rows, 8), rows)],
                dst_ref=recv.at[pl.ds(pl.multiple_of(me * rows, 8), rows)],
                send_sem=all_send.at[kind, i], recv_sem=all_recv.at[kind, i],
                device_id=dev, device_id_type=MESH,
            )
            copy.start()
            copies.append(copy)
        own = pl.ds(pl.multiple_of(me * rows, 8), rows)
        recv[own, :] = stage[own, :]
        return copies

    for load in loads:
        load.wait()
    pl.semaphore_wait(barrier, len(greeted))
    now_copies = exchange(0, sstage.at[0], srecv.at[0], 32)
    pack_y(s0)
    pack_z(s0)
    halo0 = halos(s0, 0)
    mid_copies = exchange(1, sstage.at[1], srecv.at[1], 32)

    linkf = jnp.concatenate([link[k, 0] for k in range(6)] + [jnp.zeros((2, blk), jnp.int32)], axis=0)
    over = (iota((blk, LANES), 0) == iota((blk, LANES), 1) // BS).astype(F32).astype(BF16)
    mask = dot(linkf.astype(F32).astype(BF16), over, ((1,), (0,)))
    in_blk = lane % BS
    is_lo, is_hi = in_blk == 0, in_blk == BS - 1
    zmask = jnp.where(is_lo, mask[4:5], mask[5:6]) > 0.5
    sign = jnp.where(is_lo, 0.5, -0.5)
    ends = (lane == 0) | (lane == LANES - 1)
    half_lane = (iota((8, LANES), 1) % BS) // 2
    lo8 = iota((8, LANES), 1) % BS == 0

    def expand(level):
        for c in range(chunks):
            rows = srecv[level, pl.ds(c, count, stride=16), :]
            xt[pl.ds(c * LANES, LANES), :] = dot(stacked(rows), be3, ((0,), (0,)))
        for k in range(20):
            tile = xt[pl.ds(k * 64, 8, stride=8), :]
            for b in range(1, 8):
                tile = jnp.where(half_lane == b, xt[pl.ds(k * 64 + b, 8, stride=8), :], tile)
            cxy[pl.ds(k * BS, 8, stride=2), :] = tile
            cxy[pl.ds(k * BS + 1, 8, stride=2), :] = tile
        for k in range(40):
            tile = jnp.where(lo8, xt[pl.ds(1280 + k * 8, 8), :], xt[pl.ds(1600 + k * 8, 8), :])
            cz[pl.ds(k * BS, 8, stride=2), :] = tile
            cz[pl.ds(k * BS + 1, 8, stride=2), :] = tile

    def advance(ref, step, store):
        for side in range(2):
            chosen = jnp.broadcast_to(mask[side:side + 1], (BS, LANES)) > 0.5
            for f in range(5):
                ref[f, pl.ds(side * 17 * BS, BS), :] = jnp.where(
                    chosen, hx[step, side, f], cxy[pl.ds((side * 5 + f) * BS, BS), :]
                )
        for side in range(2):
            chosen = jnp.broadcast_to(mask[2 + side:3 + side], (BS, LANES)) > 0.5
            ghost = [
                jnp.where(chosen, hy[step, side, f], cxy[pl.ds(((2 + side) * 5 + f) * BS, BS), :])
                for f in range(5)
            ]
            cells = [ref[f, pl.ds(BS + side * (BS - 1), BS, stride=BS), :] for f in range(5)]
            gf, gs = flux(ghost, prim(ghost), 1)
            cf, cs = flux(cells, prim(cells), 1)
            face = interface(ghost, gf, gs, cells, cf, cs, 0.5 if side == 0 else -0.5)
            for f in range(5):
                hyf[pl.ds((side * 5 + f) * BS, BS), :] = face[f]
        comb = []
        for k in range(2):
            left = pltpu.roll(hz[step, 0, k], 1, 1)
            right = pltpu.roll(hz[step, 1, k], LANES - 1, 1)
            comb.append(jnp.where(lane % 2 == 0, right, left))

        ul = [plane(ref, f, -1) for f in range(5)]
        u = [plane(ref, f, 0) for f in range(5)]
        fl, sl = flux(ul, prim(ul), 0)
        pr = prim(u)
        fc, sc = flux(u, pr, 0)
        first = interface(ul, fl, sl, u, fc, sc)

        def body(x, carry):
            hxl, u, pr = carry
            un = [plane(ref, f, x + 1) for f in range(5)]
            prn = prim(un)
            fc, sc = flux(u, pr, 0)
            fn, sn = flux(un, prn, 0)
            hxr = interface(u, fc, sc, un, fn, sn)
            total = [hxr[f] - hxl[f] for f in range(5)]

            fc, sc = flux(u, pr, 1)
            ub = [pltpu.roll(a, 1, 0) for a in u]
            fb = [pltpu.roll(a, 1, 0) for a in fc]
            low = interface(ub, fb, pltpu.roll(sc, 1, 0), u, fc, sc)
            for f in range(5):
                lo = jnp.where(sub == 0, hyf[pl.ds(f * BS + x, 1), :], low[f])
                hi = jnp.where(sub == BS - 1, hyf[pl.ds((5 + f) * BS + x, 1), :], pltpu.roll(low[f], BS - 1, 0))
                total[f] = total[f] + (hi - lo)

            fc, sc = flux(u, pr, 2)
            ub = [pltpu.roll(a, 1, 1) for a in u]
            fb = [pltpu.roll(a, 1, 1) for a in fc]
            low = interface(ub, fb, pltpu.roll(sc, 1, 1), u, fc, sc)
            ghost = []
            for f in range(5):
                i = (f % 4) * BS + x
                far = pltpu.roll(comb[f // 4], LANES - 1 - 2 * i, 1)
                near = jnp.where(is_lo, ub[f], pltpu.roll(u[f], LANES - 1, 1))
                near = jnp.where(ends, far, near)
                at = pl.multiple_of((f * 8 + x // 2) * BS, BS)
                ghost.append(jnp.where(zmask, near, cz[pl.ds(at, BS), :]))
            ghost = [jnp.where(is_lo | is_hi, ghost[f], u[f]) for f in range(5)]
            gf, gs = flux(ghost, prim(ghost), 2)
            edge = interface(ghost, gf, gs, u, fc, sc, sign)
            for f in range(5):
                lo = jnp.where(is_lo, edge[f], low[f])
                hi = jnp.where(is_hi, edge[f], pltpu.roll(low[f], LANES - 1, 1))
                total[f] = total[f] + (hi - lo)
                store(f, x, u[f] - LAMBDA * total[f])
            return hxr, un, prn

        lax.fori_loop(0, BS, body, (first, u, pr))

    def store_mid(f, x, value):
        s1[f, pl.ds(pl.multiple_of((x + 1) * BS, BS), BS), :] = value

    def store_out(f, x, value):
        out[f, pl.ds(pl.multiple_of(x * BS, BS), BS), :] = value

    for copy in now_copies:
        copy.wait_recv()
    expand(0)
    for copy in halo0:
        copy.wait()
    advance(s0, 0, store_mid)
    pack_y(s1)
    pack_z(s1)
    halo1 = halos(s1, 1)
    for copy in mid_copies:
        copy.wait_recv()
    expand(1)
    for copy in halo1:
        copy.wait()
    advance(s1, 1, store_out)

    for f in range(5):
        for a in range(8):
            total = None
            for x in range(2):
                for y in range(2):
                    piece = out[f, pl.ds((2 * a + x) * BS + y, 8, stride=2), :]
                    total = piece if total is None else total + piece
            xy[pl.ds((f * 8 + a) * 8, 8), :] = 0.125 * total
    used = 5 * 64
    interleave = (iota((LANES, 8 * LANES), 0) == iota((LANES, 8 * LANES), 1) // 8).astype(F32).astype(BF16)
    lane8 = iota((blk, LANES), 1) % 8
    sel = beside(sel_tk, blk)
    for c in range((used + LANES - 1) // LANES):
        size = min(LANES, used - c * LANES)
        block = xy[pl.ds(c * LANES, LANES), :]
        if size < LANES:
            block = jnp.where(iota((LANES, LANES), 0) < size, block, 0.0)
        zt[...] = block.T
        rows = jnp.concatenate(
            [zt[pl.ds(2 * z, blk, stride=BS), :] + zt[pl.ds(2 * z + 1, blk, stride=BS), :] for z in range(8)],
            axis=0,
        )
        wide = dot(jnp.concatenate(parts_of(rows, 3), axis=0).astype(BF16), interleave, ((1,), (0,)))
        wide = wide[:64] + wide[64:128] + wide[128:]
        for g in range(size // 16):
            tile = wide[0:8, g * LANES:(g + 1) * LANES]
            for z in range(1, 8):
                tile = jnp.where(lane8 == z, wide[z * 8:z * 8 + 8, g * LANES:(g + 1) * LANES], tile)
            rstage[pl.ds(c * 8 + g, count, stride=rchunks), :] = dot(sel, stacked(tile), ((1,), (0,)))
    back = exchange(2, rstage, rrecv, 2 * rchunks)
    for copy in back:
        copy.wait_recv()
    sel = beside(sel_st, count)
    for c in range(rchunks):
        rows = rrecv[pl.ds(c, count, stride=rchunks), :]
        coarse[0, :, pl.ds(c * LANES, LANES)] = dot(sel, stacked(rows), ((1,), (0,)))
    for copy in now_copies + mid_copies + back:
        copy.wait_send()


def shards(n, fine, shell, parent, link):
    group = n[1] * n[2]
    count = 2 * group
    rwidth = 5 * (BS // 2) ** 3
    fine2 = fine.reshape(5, BS * BS, LANES)
    vmem = pl.BlockSpec(memory_space=pltpu.VMEM)
    out, coarse = pl.pallas_call(
        functools.partial(kernel, n),
        out_shape=(
            jax.ShapeDtypeStruct((5, BS * BS, LANES), F32),
            jax.ShapeDtypeStruct((1, shell.shape[1], rwidth), F32),
        ),
        in_specs=[pl.BlockSpec(memory_space=pl.ANY), vmem, vmem, vmem],
        out_specs=(vmem, vmem),
        scratch_shapes=[
            pltpu.VMEM((5, 18 * BS, LANES), F32),
            pltpu.VMEM((5, 18 * BS, LANES), F32),
            pltpu.VMEM((2, 5, BS, LANES), F32),
            pltpu.VMEM((2, BS, LANES), F32),
            pltpu.VMEM((2, 2, 5, BS, LANES), F32),
            pltpu.VMEM((2, 2, 5, BS, LANES), F32),
            pltpu.VMEM((2, 2, 2, BS, LANES), F32),
            pltpu.VMEM((2, count * 16, LANES), F32),
            pltpu.VMEM((2, count * 16, LANES), F32),
            pltpu.VMEM((count * (rwidth // LANES), LANES), F32),
            pltpu.VMEM((count * (rwidth // LANES), LANES), F32),
            pltpu.VMEM((1920, LANES), F32),
            pltpu.VMEM((20 * BS, LANES), F32),
            pltpu.VMEM((40 * BS, LANES), F32),
            pltpu.VMEM((10 * BS, LANES), F32),
            pltpu.VMEM((384, LANES), F32),
            pltpu.VMEM((LANES, LANES), F32),
            pltpu.SemaphoreType.DMA((5,)),
            pltpu.SemaphoreType.DMA((2, 6)),
            pltpu.SemaphoreType.DMA((2, 6)),
            pltpu.SemaphoreType.DMA((3, group)),
            pltpu.SemaphoreType.DMA((3, group)),
        ],
        compiler_params=pltpu.CompilerParams(
            collective_id=0, has_side_effects=True, vmem_limit_bytes=32 * 1024 * 1024
        ),
    )(fine2, shell, parent, link)
    return out.reshape(fine.shape), coarse


def solution(mesh):
    n = (mesh.shape["gx"], mesh.shape["gy"], mesh.shape["gz"])
    return jax.shard_map(
        functools.partial(shards, n),
        mesh=mesh,
        in_specs=(
            P(None, "gx", "gy", "gz"),
            P("gx", ("gy", "gz"), None),
            P("gx", None),
            P(None, "gx", "gy", "gz"),
        ),
        out_specs=(P(None, "gx", "gy", "gz"), P("gx", ("gy", "gz"), None)),
        check_vma=False,
    )
```

```python
import functools

import jax
import jax.numpy as jnp
from jax import lax
from jax.experimental import pallas as pl
from jax.experimental.pallas import tpu as pltpu
from jax.sharding import PartitionSpec as P

BS = 16
GAMMA = 1.4
LAMBDA = 0.05
LANES = 128
MESH = pl.DeviceIdType.MESH
F32 = jnp.float32
BF16 = jnp.bfloat16


def iota(shape, dim):
    return lax.broadcasted_iota(jnp.int32, shape, dim)


def parts_of(x, count):
    result = []
    for _ in range(count - 1):
        head = x.astype(BF16).astype(F32)
        result.append(head)
        x = x - head
    result.append(x)
    return result


def dot(a, b, contract):
    return lax.dot_general(a, b, (contract, ((), ())), preferred_element_type=F32)


def stacked(x):
    pieces = parts_of(x, 3)
    if x.shape[0] % 16:
        pieces.append(jnp.zeros_like(x))
    return jnp.concatenate(pieces, axis=0).astype(BF16)


def beside(x, rows):
    count = 4 if rows % 16 else 3
    return jnp.concatenate([x] * count, axis=1).astype(BF16)


def prim(u):
    inv = 1.0 / u[0]
    vel = [u[1] * inv, u[2] * inv, u[3] * inv]
    press = (GAMMA - 1.0) * (u[4] - 0.5 * (u[1] * vel[0] + u[2] * vel[1] + u[3] * vel[2]))
    sound = jnp.sqrt(GAMMA * press * inv)
    return vel, press, sound


def flux(u, pr, d):
    vel, press, sound = pr
    vd = vel[d]
    f = [u[1 + d], u[1] * vd, u[2] * vd, u[3] * vd, (u[4] + press) * vd]
    f[1 + d] = f[1 + d] + press
    return f, jnp.abs(vd) + sound


def interface(ul, fl, sl, ur, fr, sr, sign=0.5):
    wave = sign * jnp.maximum(sl, sr)
    return [0.5 * (fl[i] + fr[i]) - wave * (ur[i] - ul[i]) for i in range(5)]


def kernel(
    n,
    fine, shell_hbm, parent_hbm, link_hbm, out_hbm, coarse,
    out, shell, parent, link, s0, s1, ypack, zpack, hx, hy, hz, sstage, srecv, rstage, rrecv, xt, cxy, cz, hyf, xy, zt,
    load_sem, halo_send, halo_recv, all_send, all_recv,
):
    nx, ny, nz = n
    group = ny * nz
    count = 2 * group
    gx, gy, gz = lax.axis_index("gx"), lax.axis_index("gy"), lax.axis_index("gz")
    me = gy * nz + gz
    blk = shell.shape[1]
    width = shell.shape[2] // 2
    chunks = width // LANES
    rwidth = coarse.shape[2]
    rchunks = rwidth // LANES
    nq = parent.shape[1]
    peers = []
    for i in range(1, group):
        peer = lax.rem(me + i, group)
        peers.append((gx, peer // nz, lax.rem(peer, nz)))
    xlo, xhi = (lax.rem(gx + nx - 1, nx), gy, gz), (lax.rem(gx + 1, nx), gy, gz)
    ylo, yhi = (gx, lax.rem(gy + ny - 1, ny), gz), (gx, lax.rem(gy + 1, ny), gz)
    zlo, zhi = (gx, gy, lax.rem(gz + nz - 1, nz)), (gx, gy, lax.rem(gz + 1, nz))

    barrier = pltpu.get_barrier_semaphore()
    greeted = peers + [xlo, xhi]
    for dev in greeted:
        pl.semaphore_signal(barrier, inc=1, device_id=dev, device_id_type=MESH)

    loads = []
    for k, (src, dst) in enumerate(((parent_hbm, parent), (shell_hbm, shell), (link_hbm, link))):
        load = pltpu.make_async_copy(src, dst, load_sem.at[5 + k])
        load.start()
        loads.append(load)
    for f in range(5):
        load = pltpu.make_async_copy(fine.at[f], s0.at[f, pl.ds(BS, BS * BS)], load_sem.at[f])
        load.start()
        loads.append(load)

    loads[0].wait()
    par = parent[...]
    lane_q = iota((1, nq), 1)
    owner = par // blk
    rank = jnp.zeros((1, nq), jnp.int32)
    for j in range(1, blk):
        before = pltpu.roll(jnp.broadcast_to(owner, (8, nq)), j, 1)[0:1]
        rank = rank + jnp.where((lane_q % blk >= j) & (before == owner), 1, 0)
    at_owner = (lane_q // blk) * 2 + rank
    at_block = owner * 2 + rank
    to_t = (jnp.broadcast_to(at_owner, (count, nq)) == iota((count, nq), 0)).astype(F32).astype(BF16)
    mine = (jnp.broadcast_to(par, (blk, nq)) == me * blk + iota((blk, nq), 0)).astype(F32).astype(BF16)
    sel_ts = dot(to_t, mine, ((1,), (1,)))
    sel_st = dot(mine, to_t, ((1,), (1,)))
    at_block8 = jnp.broadcast_to(at_block.astype(F32), (8, nq)).astype(BF16)
    spread = (iota((nq, LANES), 0) == me * blk + iota((nq, LANES), 1) // BS).astype(F32).astype(BF16)
    pick = (iota((nq, blk), 0) == me * blk + iota((nq, blk), 1)).astype(F32).astype(BF16)
    row_lane = dot(at_block8, spread, ((1,), (0,)))[0:1]
    row_blk = dot(at_block8, pick, ((1,), (0,)))[0:1]
    be = (jnp.broadcast_to(row_lane, (count, LANES)) == iota((count, LANES), 0).astype(F32)).astype(F32)
    be3 = jnp.concatenate([be] * 3, axis=0).astype(BF16)
    sel_tk = (jnp.broadcast_to(row_blk, (count, blk)) == iota((count, blk), 0).astype(F32)).astype(F32)

    loads[1].wait()
    sel = beside(sel_ts, blk)
    for c in range(chunks):
        now = shell[0, :, pl.ds(c * LANES, LANES)]
        end = shell[0, :, pl.ds(width + c * LANES, LANES)]
        both = jnp.concatenate([stacked(now), stacked(0.5 * (now + end))], axis=1)
        rows = dot(sel, both, ((1,), (0,)))
        sstage[0, pl.ds(c, count, stride=16), :] = rows[:, :LANES]
        sstage[1, pl.ds(c, count, stride=16), :] = rows[:, LANES:]

    lane = iota((BS, LANES), 1)
    sub = iota((BS, LANES), 0)

    def plane(ref, f, x):
        return ref[f, pl.ds(pl.multiple_of((x + 1) * BS, BS), BS), :]

    def pack_y(ref):
        for f in range(5):
            ypack[0, f] = ref[f, pl.ds(BS, BS, stride=BS), :]
            ypack[1, f] = ref[f, pl.ds(2 * BS - 1, BS, stride=BS), :]

    def pack_z(ref):
        def body(x, acc):
            a0, a1 = acc
            for f in range(4):
                i = f * BS + x
                a0 = jnp.where(lane // 2 == i, pltpu.roll(plane(ref, f, x), 2 * i + 1, 1), a0)
            a1 = jnp.where(lane // 2 == x, pltpu.roll(plane(ref, 4, x), 2 * x + 1, 1), a1)
            return a0, a1

        zero = jnp.zeros((BS, LANES), F32)
        a0, a1 = lax.fori_loop(0, BS, body, (zero, zero), unroll=True)
        zpack[0] = a0
        zpack[1] = a1

    def halos(ref, step):
        def send(k, src, dst, dev):
            copy = pltpu.make_async_remote_copy(
                src_ref=src, dst_ref=dst, send_sem=halo_send.at[step, k], recv_sem=halo_recv.at[step, k],
                device_id=dev, device_id_type=MESH,
            )
            copy.start()
            return copy

        return [
            send(0, ref.at[:, pl.ds(BS * BS, BS)], hx.at[step, 0], xhi),
            send(1, ref.at[:, pl.ds(BS, BS)], hx.at[step, 1], xlo),
            send(2, ypack.at[1], hy.at[step, 0], yhi),
            send(3, ypack.at[0], hy.at[step, 1], ylo),
            send(4, zpack, hz.at[step, 0], zhi),
            send(5, zpack, hz.at[step, 1], zlo),
        ]

    def exchange(kind, stage, recv, rows):
        copies = []
        for i, dev in enumerate(peers):
            to = lax.rem(me + i + 1, group)
            copy = pltpu.make_async_remote_copy(
                src_ref=stage.at[pl.ds(pl.multiple_of(to * rows, 8), rows)],
                dst_ref=recv.at[pl.ds(pl.multiple_of(me * rows, 8), rows)],
                send_sem=all_send.at[kind, i], recv_sem=all_recv.at[kind, i],
                device_id=dev, device_id_type=MESH,
            )
            copy.start()
            copies.append(copy)
        own = pl.ds(pl.multiple_of(me * rows, 8), rows)
        recv[own, :] = stage[own, :]
        return copies

    for load in loads[2:]:
        load.wait()
    pl.semaphore_wait(barrier, len(greeted))
    now_copies = exchange(0, sstage.at[0], srecv.at[0], 32)
    pack_y(s0)
    pack_z(s0)
    halo0 = halos(s0, 0)
    mid_copies = exchange(1, sstage.at[1], srecv.at[1], 32)

    linkf = jnp.concatenate([link[k, 0] for k in range(6)] + [jnp.zeros((2, blk), jnp.int32)], axis=0)
    over = (iota((blk, LANES), 0) == iota((blk, LANES), 1) // BS).astype(F32).astype(BF16)
    mask = dot(linkf.astype(F32).astype(BF16), over, ((1,), (0,)))
    in_blk = lane % BS
    is_lo, is_hi = in_blk == 0, in_blk == BS - 1
    zmask = jnp.where(is_lo, mask[4:5], mask[5:6]) > 0.5
    sign = jnp.where(is_lo, 0.5, -0.5)
    ends = (lane == 0) | (lane == LANES - 1)
    half_lane = (iota((8, LANES), 1) % BS) // 2
    lo8 = iota((8, LANES), 1) % BS == 0

    def expand(level):
        for c in range(chunks):
            rows = srecv[level, pl.ds(c, count, stride=16), :]
            xt[pl.ds(c * LANES, LANES), :] = dot(stacked(rows), be3, ((0,), (0,)))
        for k in range(20):
            tile = xt[pl.ds(k * 64, 8, stride=8), :]
            for b in range(1, 8):
                tile = jnp.where(half_lane == b, xt[pl.ds(k * 64 + b, 8, stride=8), :], tile)
            cxy[pl.ds(k * BS, 8, stride=2), :] = tile
            cxy[pl.ds(k * BS + 1, 8, stride=2), :] = tile
        for k in range(40):
            tile = jnp.where(lo8, xt[pl.ds(1280 + k * 8, 8), :], xt[pl.ds(1600 + k * 8, 8), :])
            cz[pl.ds(k * BS, 8, stride=2), :] = tile
            cz[pl.ds(k * BS + 1, 8, stride=2), :] = tile

    def advance(ref, step, store):
        for side in range(2):
            chosen = jnp.broadcast_to(mask[side:side + 1], (BS, LANES)) > 0.5
            for f in range(5):
                ref[f, pl.ds(side * 17 * BS, BS), :] = jnp.where(
                    chosen, hx[step, side, f], cxy[pl.ds((side * 5 + f) * BS, BS), :]
                )
        for side in range(2):
            chosen = jnp.broadcast_to(mask[2 + side:3 + side], (BS, LANES)) > 0.5
            ghost = [
                jnp.where(chosen, hy[step, side, f], cxy[pl.ds(((2 + side) * 5 + f) * BS, BS), :])
                for f in range(5)
            ]
            cells = [ref[f, pl.ds(BS + side * (BS - 1), BS, stride=BS), :] for f in range(5)]
            gf, gs = flux(ghost, prim(ghost), 1)
            cf, cs = flux(cells, prim(cells), 1)
            face = interface(ghost, gf, gs, cells, cf, cs, 0.5 if side == 0 else -0.5)
            for f in range(5):
                hyf[pl.ds((side * 5 + f) * BS, BS), :] = face[f]
        comb = []
        for k in range(2):
            left = pltpu.roll(hz[step, 0, k], 1, 1)
            right = pltpu.roll(hz[step, 1, k], LANES - 1, 1)
            comb.append(jnp.where(lane % 2 == 0, right, left))

        ul = [plane(ref, f, -1) for f in range(5)]
        u = [plane(ref, f, 0) for f in range(5)]
        fl, sl = flux(ul, prim(ul), 0)
        pr = prim(u)
        fc, sc = flux(u, pr, 0)
        first = interface(ul, fl, sl, u, fc, sc)

        def body(x, carry):
            hxl, u, pr = carry
            un = [plane(ref, f, x + 1) for f in range(5)]
            prn = prim(un)
            fc, sc = flux(u, pr, 0)
            fn, sn = flux(un, prn, 0)
            hxr = interface(u, fc, sc, un, fn, sn)
            total = [hxr[f] - hxl[f] for f in range(5)]

            fc, sc = flux(u, pr, 1)
            ub = [pltpu.roll(a, 1, 0) for a in u]
            fb = [pltpu.roll(a, 1, 0) for a in fc]
            low = interface(ub, fb, pltpu.roll(sc, 1, 0), u, fc, sc)
            for f in range(5):
                lo = jnp.where(sub == 0, hyf[pl.ds(f * BS + x, 1), :], low[f])
                hi = jnp.where(sub == BS - 1, hyf[pl.ds((5 + f) * BS + x, 1), :], pltpu.roll(low[f], BS - 1, 0))
                total[f] = total[f] + (hi - lo)

            fc, sc = flux(u, pr, 2)
            ub = [pltpu.roll(a, 1, 1) for a in u]
            fb = [pltpu.roll(a, 1, 1) for a in fc]
            low = interface(ub, fb, pltpu.roll(sc, 1, 1), u, fc, sc)
            ghost = []
            for f in range(5):
                i = (f % 4) * BS + x
                far = pltpu.roll(comb[f // 4], LANES - 1 - 2 * i, 1)
                near = jnp.where(is_lo, ub[f], pltpu.roll(u[f], LANES - 1, 1))
                near = jnp.where(ends, far, near)
                at = pl.multiple_of((f * 8 + x // 2) * BS, BS)
                ghost.append(jnp.where(zmask, near, cz[pl.ds(at, BS), :]))
            ghost = [jnp.where(is_lo | is_hi, ghost[f], u[f]) for f in range(5)]
            gf, gs = flux(ghost, prim(ghost), 2)
            edge = interface(ghost, gf, gs, u, fc, sc, sign)
            for f in range(5):
                lo = jnp.where(is_lo, edge[f], low[f])
                hi = jnp.where(is_hi, edge[f], pltpu.roll(low[f], LANES - 1, 1))
                total[f] = total[f] + (hi - lo)
                store(f, x, u[f] - LAMBDA * total[f])
            return hxr, un, prn

        lax.fori_loop(0, BS, body, (first, u, pr), unroll=2)

    def store_mid(f, x, value):
        s1[f, pl.ds(pl.multiple_of((x + 1) * BS, BS), BS), :] = value

    def store_out(f, x, value):
        out[f, pl.ds(pl.multiple_of(x * BS, BS), BS), :] = value

    for copy in now_copies:
        copy.wait_recv()
    expand(0)
    for copy in halo0:
        copy.wait()
    advance(s0, 0, store_mid)
    pack_y(s1)
    pack_z(s1)
    halo1 = halos(s1, 1)
    for copy in mid_copies:
        copy.wait_recv()
    expand(1)
    for copy in halo1:
        copy.wait()
    advance(s1, 1, store_out)
    result = pltpu.make_async_copy(out, out_hbm, load_sem.at[8])
    result.start()

    for f in range(5):
        for a in range(8):
            total = None
            for x in range(2):
                for y in range(2):
                    piece = out[f, pl.ds((2 * a + x) * BS + y, 8, stride=2), :]
                    total = piece if total is None else total + piece
            xy[pl.ds((f * 8 + a) * 8, 8), :] = 0.125 * total
    used = 5 * 64
    interleave = (iota((LANES, 8 * LANES), 0) == iota((LANES, 8 * LANES), 1) // 8).astype(F32).astype(BF16)
    lane8 = iota((blk, LANES), 1) % 8
    sel = beside(sel_tk, blk)
    for c in range((used + LANES - 1) // LANES):
        size = min(LANES, used - c * LANES)
        block = xy[pl.ds(c * LANES, LANES), :]
        if size < LANES:
            block = jnp.where(iota((LANES, LANES), 0) < size, block, 0.0)
        zt[...] = block.T
        rows = jnp.concatenate(
            [zt[pl.ds(2 * z, blk, stride=BS), :] + zt[pl.ds(2 * z + 1, blk, stride=BS), :] for z in range(8)],
            axis=0,
        )
        wide = dot(jnp.concatenate(parts_of(rows, 3), axis=0).astype(BF16), interleave, ((1,), (0,)))
        wide = wide[:64] + wide[64:128] + wide[128:]
        for g in range(size // 16):
            tile = wide[0:8, g * LANES:(g + 1) * LANES]
            for z in range(1, 8):
                tile = jnp.where(lane8 == z, wide[z * 8:z * 8 + 8, g * LANES:(g + 1) * LANES], tile)
            rstage[pl.ds(c * 8 + g, count, stride=rchunks), :] = dot(sel, stacked(tile), ((1,), (0,)))
    back = exchange(2, rstage, rrecv, 2 * rchunks)
    for copy in back:
        copy.wait_recv()
    sel = beside(sel_st, count)
    for c in range(rchunks):
        rows = rrecv[pl.ds(c, count, stride=rchunks), :]
        coarse[0, :, pl.ds(c * LANES, LANES)] = dot(sel, stacked(rows), ((1,), (0,)))
    for copy in now_copies + mid_copies + back:
        copy.wait_send()
    result.wait()


def shards(n, fine, shell, parent, link):
    group = n[1] * n[2]
    count = 2 * group
    rwidth = 5 * (BS // 2) ** 3
    fine2 = fine.reshape(5, BS * BS, LANES)
    vmem = pl.BlockSpec(memory_space=pltpu.VMEM)
    out, coarse = pl.pallas_call(
        functools.partial(kernel, n),
        out_shape=(
            jax.ShapeDtypeStruct((5, BS * BS, LANES), F32),
            jax.ShapeDtypeStruct((1, shell.shape[1], rwidth), F32),
        ),
        in_specs=[pl.BlockSpec(memory_space=pltpu.HBM)] * 4,
        out_specs=(pl.BlockSpec(memory_space=pltpu.HBM), vmem),
        scratch_shapes=[
            pltpu.VMEM((5, BS * BS, LANES), F32),
            pltpu.VMEM(shell.shape, F32),
            pltpu.VMEM(parent.shape, jnp.int32),
            pltpu.VMEM(link.shape, jnp.int32),
            pltpu.VMEM((5, 18 * BS, LANES), F32),
            pltpu.VMEM((5, 18 * BS, LANES), F32),
            pltpu.VMEM((2, 5, BS, LANES), F32),
            pltpu.VMEM((2, BS, LANES), F32),
            pltpu.VMEM((2, 2, 5, BS, LANES), F32),
            pltpu.VMEM((2, 2, 5, BS, LANES), F32),
            pltpu.VMEM((2, 2, 2, BS, LANES), F32),
            pltpu.VMEM((2, count * 16, LANES), F32),
            pltpu.VMEM((2, count * 16, LANES), F32),
            pltpu.VMEM((count * (rwidth // LANES), LANES), F32),
            pltpu.VMEM((count * (rwidth // LANES), LANES), F32),
            pltpu.VMEM((1920, LANES), F32),
            pltpu.VMEM((20 * BS, LANES), F32),
            pltpu.VMEM((40 * BS, LANES), F32),
            pltpu.VMEM((10 * BS, LANES), F32),
            pltpu.VMEM((384, LANES), F32),
            pltpu.VMEM((LANES, LANES), F32),
            pltpu.SemaphoreType.DMA((9,)),
            pltpu.SemaphoreType.DMA((2, 6)),
            pltpu.SemaphoreType.DMA((2, 6)),
            pltpu.SemaphoreType.DMA((3, group)),
            pltpu.SemaphoreType.DMA((3, group)),
        ],
        compiler_params=pltpu.CompilerParams(
            collective_id=0, has_side_effects=True, vmem_limit_bytes=62 * 1024 * 1024
        ),
    )(fine2, shell, parent, link)
    return out.reshape(fine.shape), coarse


def solution(mesh):
    n = (mesh.shape["gx"], mesh.shape["gy"], mesh.shape["gz"])
    return jax.shard_map(
        functools.partial(shards, n),
        mesh=mesh,
        in_specs=(
            P(None, "gx", "gy", "gz"),
            P("gx", ("gy", "gz"), None),
            P("gx", None),
            P(None, "gx", "gy", "gz"),
        ),
        out_specs=(P(None, "gx", "gy", "gz"), P("gx", ("gy", "gz"), None)),
        check_vma=False,
    )
```

```python
import functools

import jax
import jax.numpy as jnp
from jax import lax
from jax.experimental import pallas as pl
from jax.experimental.pallas import tpu as pltpu
from jax.sharding import PartitionSpec as P

BS = 16
GAMMA = 1.4
LAMBDA = 0.05
LANES = 128
MESH = pl.DeviceIdType.MESH
F32 = jnp.float32
BF16 = jnp.bfloat16


def iota(shape, dim):
    return lax.broadcasted_iota(jnp.int32, shape, dim)


def parts_of(x, count):
    result = []
    for _ in range(count - 1):
        head = x.astype(BF16).astype(F32)
        result.append(head)
        x = x - head
    result.append(x)
    return result


def dot(a, b, contract):
    return lax.dot_general(a, b, (contract, ((), ())), preferred_element_type=F32)


def stacked(x):
    pieces = parts_of(x, 3)
    if x.shape[0] % 16:
        pieces.append(jnp.zeros_like(x))
    return jnp.concatenate(pieces, axis=0).astype(BF16)


def beside(x, rows):
    count = 4 if rows % 16 else 3
    return jnp.concatenate([x] * count, axis=1).astype(BF16)


def prim(u):
    inv = 1.0 / u[0]
    vel = [u[1] * inv, u[2] * inv, u[3] * inv]
    press = (GAMMA - 1.0) * (u[4] - 0.5 * (u[1] * vel[0] + u[2] * vel[1] + u[3] * vel[2]))
    sound = jnp.sqrt(GAMMA * press * inv)
    return vel, press, sound


def flux(u, pr, d):
    vel, press, sound = pr
    vd = vel[d]
    f = [u[1 + d], u[1] * vd, u[2] * vd, u[3] * vd, (u[4] + press) * vd]
    f[1 + d] = f[1 + d] + press
    return f, jnp.abs(vd) + sound


def interface(ul, fl, sl, ur, fr, sr, sign=0.5):
    wave = sign * jnp.maximum(sl, sr)
    return [0.5 * (fl[i] + fr[i]) - wave * (ur[i] - ul[i]) for i in range(5)]


def kernel(
    n,
    fine, shell_hbm, parent_hbm, link_hbm, out_hbm, coarse,
    out, shell, parent, link, s0, s1, ypack, zpack, hx, hy, hz, sstage, srecv, rstage, rrecv, xt, cxy, cz, cells_z, xy, zt,
    load_sem, halo_send, halo_recv, all_send, all_recv,
):
    nx, ny, nz = n
    group = ny * nz
    count = 2 * group
    gx, gy, gz = lax.axis_index("gx"), lax.axis_index("gy"), lax.axis_index("gz")
    me = gy * nz + gz
    blk = shell.shape[1]
    width = shell.shape[2] // 2
    chunks = width // LANES
    rwidth = coarse.shape[2]
    rchunks = rwidth // LANES
    nq = parent.shape[1]
    peers = []
    for i in range(1, group):
        peer = lax.rem(me + i, group)
        peers.append((gx, peer // nz, lax.rem(peer, nz)))
    xlo, xhi = (lax.rem(gx + nx - 1, nx), gy, gz), (lax.rem(gx + 1, nx), gy, gz)
    ylo, yhi = (gx, lax.rem(gy + ny - 1, ny), gz), (gx, lax.rem(gy + 1, ny), gz)
    zlo, zhi = (gx, gy, lax.rem(gz + nz - 1, nz)), (gx, gy, lax.rem(gz + 1, nz))

    barrier = pltpu.get_barrier_semaphore()
    greeted = peers + [xlo, xhi]
    for dev in greeted:
        pl.semaphore_signal(barrier, inc=1, device_id=dev, device_id_type=MESH)

    loads = []
    for k, (src, dst) in enumerate(((parent_hbm, parent), (shell_hbm, shell), (link_hbm, link))):
        load = pltpu.make_async_copy(src, dst, load_sem.at[5 + k])
        load.start()
        loads.append(load)
    for f in range(5):
        load = pltpu.make_async_copy(fine.at[f], s0.at[f], load_sem.at[f])
        load.start()
        loads.append(load)

    loads[0].wait()
    par = parent[...]
    lane_q = iota((1, nq), 1)
    owner = par // blk
    rank = jnp.zeros((1, nq), jnp.int32)
    for j in range(1, blk):
        before = pltpu.roll(jnp.broadcast_to(owner, (8, nq)), j, 1)[0:1]
        rank = rank + jnp.where((lane_q % blk >= j) & (before == owner), 1, 0)
    at_owner = (lane_q // blk) * 2 + rank
    at_block = owner * 2 + rank
    to_t = (jnp.broadcast_to(at_owner, (count, nq)) == iota((count, nq), 0)).astype(F32).astype(BF16)
    mine = (jnp.broadcast_to(par, (blk, nq)) == me * blk + iota((blk, nq), 0)).astype(F32).astype(BF16)
    sel_ts = dot(to_t, mine, ((1,), (1,)))
    sel_st = dot(mine, to_t, ((1,), (1,)))
    at_block8 = jnp.broadcast_to(at_block.astype(F32), (8, nq)).astype(BF16)
    spread = (iota((nq, LANES), 0) == me * blk + iota((nq, LANES), 1) // BS).astype(F32).astype(BF16)
    pick = (iota((nq, blk), 0) == me * blk + iota((nq, blk), 1)).astype(F32).astype(BF16)
    row_lane = dot(at_block8, spread, ((1,), (0,)))[0:1]
    block_hi = ((iota((nq, LANES), 1) + 1) // BS + blk - 1) % blk
    spread_hi = (iota((nq, LANES), 0) == me * blk + block_hi).astype(F32).astype(BF16)
    row_lane_hi = dot(at_block8, spread_hi, ((1,), (0,)))[0:1]
    row_blk = dot(at_block8, pick, ((1,), (0,)))[0:1]
    be = (jnp.broadcast_to(row_lane, (count, LANES)) == iota((count, LANES), 0).astype(F32)).astype(F32)
    be3 = jnp.concatenate([be] * 3, axis=0).astype(BF16)
    be_hi = (jnp.broadcast_to(row_lane_hi, (count, LANES)) == iota((count, LANES), 0).astype(F32)).astype(F32)
    be3_hi = jnp.concatenate([be_hi] * 3, axis=0).astype(BF16)
    sel_tk = (jnp.broadcast_to(row_blk, (count, blk)) == iota((count, blk), 0).astype(F32)).astype(F32)

    loads[1].wait()
    sel = beside(sel_ts, blk)
    for c in range(chunks):
        now = shell[0, :, pl.ds(c * LANES, LANES)]
        end = shell[0, :, pl.ds(width + c * LANES, LANES)]
        both = jnp.concatenate([stacked(now), stacked(0.5 * (now + end))], axis=1)
        rows = dot(sel, both, ((1,), (0,)))
        sstage[0, pl.ds(c, count, stride=16), :] = rows[:, :LANES]
        sstage[1, pl.ds(c, count, stride=16), :] = rows[:, LANES:]

    lane = iota((BS, LANES), 1)
    sub = iota((BS, LANES), 0)
    even = lane % 2 == 0
    pair = ((lane + 1) // 2) % 8
    first_pairs = (lane + 1) % LANES < 16

    def plane(ref, f, x):
        return ref[f, pl.ds(x * BS, BS), :]

    def pack_y(ref):
        for f in range(5):
            ypack[0, f] = ref[f, pl.ds(0, BS, stride=BS), :]
            ypack[1, f] = ref[f, pl.ds(BS - 1, BS, stride=BS), :]

    def pack_z(ref):
        packed = [jnp.zeros((BS, LANES), F32)] * 2
        for f in range(5):
            for g in range(2):
                tile = plane(ref, f, 8 * g)
                for x in range(1, 8):
                    tile = jnp.where(pair == x, pltpu.roll(plane(ref, f, 8 * g + x), 2 * x, 1), tile)
                k = f * 2 + g
                cells_z[k] = tile
                moved = tile if k % 8 == 0 else pltpu.roll(tile, 16 * (k % 8), 1)
                packed[k // 8] = jnp.where(((lane + 1) // 16) % 8 == k % 8, moved, packed[k // 8])
        zpack[0] = packed[0]
        zpack[1] = packed[1]

    def halos(ref, step):
        def send(k, src, dst, dev):
            copy = pltpu.make_async_remote_copy(
                src_ref=src, dst_ref=dst, send_sem=halo_send.at[step, k], recv_sem=halo_recv.at[step, k],
                device_id=dev, device_id_type=MESH,
            )
            copy.start()
            return copy

        return [
            send(0, ref.at[:, pl.ds(BS * BS - BS, BS)], hx.at[step, 0], xhi),
            send(1, ref.at[:, pl.ds(0, BS)], hx.at[step, 1], xlo),
            send(2, ypack.at[1], hy.at[step, 0], yhi),
            send(3, ypack.at[0], hy.at[step, 1], ylo),
            send(4, zpack, hz.at[step, 0], zhi),
            send(5, zpack, hz.at[step, 1], zlo),
        ]

    def exchange(kind, stage, recv, rows):
        copies = []
        for i, dev in enumerate(peers):
            to = lax.rem(me + i + 1, group)
            copy = pltpu.make_async_remote_copy(
                src_ref=stage.at[pl.ds(pl.multiple_of(to * rows, 8), rows)],
                dst_ref=recv.at[pl.ds(pl.multiple_of(me * rows, 8), rows)],
                send_sem=all_send.at[kind, i], recv_sem=all_recv.at[kind, i],
                device_id=dev, device_id_type=MESH,
            )
            copy.start()
            copies.append(copy)
        own = pl.ds(pl.multiple_of(me * rows, 8), rows)
        recv[own, :] = stage[own, :]
        return copies

    for load in loads[2:]:
        load.wait()
    pl.semaphore_wait(barrier, len(greeted))
    now_copies = exchange(0, sstage.at[0], srecv.at[0], 32)
    pack_y(s0)
    pack_z(s0)
    halo0 = halos(s0, 0)
    mid_copies = exchange(1, sstage.at[1], srecv.at[1], 32)

    linkf = jnp.concatenate([link[k, 0] for k in range(6)] + [jnp.zeros((2, blk), jnp.int32)], axis=0)
    over = (iota((blk, LANES), 0) == iota((blk, LANES), 1) // BS).astype(F32).astype(BF16)
    over_hi = (iota((blk, LANES), 0) == ((iota((blk, LANES), 1) + 1) // BS + blk - 1) % blk).astype(F32).astype(BF16)
    linkb = linkf.astype(F32).astype(BF16)
    mask = dot(linkb, over, ((1,), (0,)))
    mask_hi = dot(linkb, over_hi, ((1,), (0,)))
    is_lo = lane % BS == 0
    at_end = is_lo | (lane % BS == BS - 1)
    zmask = jnp.where(even, mask[4:5], mask_hi[5:6]) > 0.5
    half_lane = (iota((8, LANES), 1) % BS) // 2
    even8 = iota((8, LANES), 1) % 2 == 0
    pair8 = (((iota((8, LANES), 1) + 1) // 2) % 8) // 2

    def expand(level):
        for c in range(chunks):
            rows = stacked(srecv[level, pl.ds(c, count, stride=16), :])
            if c * LANES < 1600:
                xt[pl.ds(c * LANES, LANES), :] = dot(rows, be3, ((0,), (0,)))
            if (c + 1) * LANES > 1600:
                skip = max(0, 1600 - c * LANES)
                xt[pl.ds(c * LANES + skip, LANES - skip), :] = dot(rows, be3_hi, ((0,), (0,)))[skip:]
        for k in range(20):
            tile = xt[pl.ds(k * 64, 8, stride=8), :]
            for b in range(1, 8):
                tile = jnp.where(half_lane == b, xt[pl.ds(k * 64 + b, 8, stride=8), :], tile)
            cxy[pl.ds(k * BS, 8, stride=2), :] = tile
            cxy[pl.ds(k * BS + 1, 8, stride=2), :] = tile
        for k in range(10):
            tile = None
            for a in range(4):
                at = ((k // 2) * 8 + 4 * (k % 2) + a) * 8
                piece = jnp.where(even8, xt[pl.ds(1280 + at, 8), :], xt[pl.ds(1600 + at, 8), :])
                tile = piece if a == 0 else jnp.where(pair8 == a, piece, tile)
            cz[pl.ds(k * BS, 8, stride=2), :] = tile
            cz[pl.ds(k * BS + 1, 8, stride=2), :] = tile

    def inner(ref, dst):
        def step_x(x, hxl, u, pr, last):
            if last:
                total = [-hxl[f] for f in range(5)]
                hxr, un, prn = hxl, u, pr
            else:
                at = pl.multiple_of((x + 1) * BS, BS)
                un = [ref[f, pl.ds(at, BS), :] for f in range(5)]
                prn = prim(un)
                fc, sc = flux(u, pr, 0)
                fn, sn = flux(un, prn, 0)
                hxr = interface(u, fc, sc, un, fn, sn)
                total = [hxr[f] - hxl[f] for f in range(5)]
            for d, axis, edge in ((1, 0, sub == 0), (2, 1, is_lo)):
                fc, sc = flux(u, pr, d)
                ub = [pltpu.roll(a, 1, axis) for a in u]
                fb = [pltpu.roll(a, 1, axis) for a in fc]
                low = interface(ub, fb, pltpu.roll(sc, 1, axis), u, fc, sc)
                for f in range(5):
                    lo = jnp.where(edge, 0.0, low[f])
                    total[f] = total[f] + (pltpu.roll(lo, lo.shape[axis] - 1, axis) - lo)
            at = pl.multiple_of(x * BS, BS)
            for f in range(5):
                dst[f, pl.ds(at, BS), :] = u[f] - LAMBDA * total[f]
            return hxr, un, prn

        u = [plane(ref, f, 0) for f in range(5)]
        zero = [jnp.zeros((BS, LANES), F32)] * 5
        carry = lax.fori_loop(
            0, BS - 1, lambda x, carry: step_x(x, *carry, False), (zero, u, prim(u)), unroll=3
        )
        step_x(BS - 1, *carry, True)

    def faces(ghost, cells, d, sign):
        gf, gs = flux(ghost, prim(ghost), d)
        cf, cs = flux(cells, prim(cells), d)
        return interface(ghost, gf, gs, cells, cf, cs, sign)

    def outer(ref, dst, step):
        for d in range(2):
            for side in range(2):
                chosen = jnp.broadcast_to(mask[2 * d + side:2 * d + side + 1], (BS, LANES)) > 0.5
                halo = hx if d == 0 else hy
                if d == 0:
                    rows = pl.ds(side * (BS - 1) * BS, BS)
                else:
                    rows = pl.ds(side * (BS - 1), BS, stride=BS)
                ghost = [
                    jnp.where(chosen, halo[step, side, f], cxy[pl.ds(((2 * d + side) * 5 + f) * BS, BS), :])
                    for f in range(5)
                ]
                cells = [ref[f, rows, :] for f in range(5)]
                face = faces(ghost, cells, d, 0.5 - side)
                for f in range(5):
                    dst[f, rows, :] = dst[f, rows, :] + (LAMBDA - 2 * side * LAMBDA) * face[f]
        comb = []
        for k in range(2):
            left = pltpu.roll(hz[step, 0, k], 1, 1)
            right = pltpu.roll(hz[step, 1, k], LANES - 1, 1)
            comb.append(jnp.where(even, left, right))
        sign = jnp.where(even, 0.5, -0.5)
        scale = jnp.where(even, LAMBDA, -LAMBDA)
        for g in range(2):
            cells, ghost = [], []
            for f in range(5):
                k = f * 2 + g
                tile = cells_z[k]
                near = jnp.where(even, pltpu.roll(tile, 1, 1), pltpu.roll(tile, LANES - 1, 1))
                far = comb[k // 8]
                if k % 8:
                    far = pltpu.roll(far, LANES - 16 * (k % 8), 1)
                fine_side = jnp.where(first_pairs, far, near)
                cells.append(tile)
                ghost.append(jnp.where(zmask, fine_side, cz[pl.ds(k * BS, BS), :]))
            face = faces(ghost, cells, 2, sign)
            for f in range(5):
                change = scale * face[f]
                for x in range(8):
                    moved = change if x == 0 else pltpu.roll(change, LANES - 2 * x, 1)
                    rows = pl.ds((8 * g + x) * BS, BS)
                    dst[f, rows, :] = dst[f, rows, :] + jnp.where(at_end, moved, 0.0)

    inner(s0, s1)
    for copy in now_copies:
        copy.wait_recv()
    expand(0)
    for copy in halo0:
        copy.wait()
    outer(s0, s1, 0)
    pack_y(s1)
    pack_z(s1)
    halo1 = halos(s1, 1)
    for copy in mid_copies:
        copy.wait_recv()
    expand(1)
    inner(s1, out)
    for copy in halo1:
        copy.wait()
    outer(s1, out, 1)
    result = pltpu.make_async_copy(out, out_hbm, load_sem.at[8])
    result.start()

    for f in range(5):
        for a in range(8):
            total = None
            for x in range(2):
                for y in range(2):
                    piece = out[f, pl.ds((2 * a + x) * BS + y, 8, stride=2), :]
                    total = piece if total is None else total + piece
            xy[pl.ds((f * 8 + a) * 8, 8), :] = 0.125 * total
    used = 5 * 64
    interleave = (iota((LANES, 8 * LANES), 0) == iota((LANES, 8 * LANES), 1) // 8).astype(F32).astype(BF16)
    lane8 = iota((blk, LANES), 1) % 8
    sel = beside(sel_tk, blk)
    for c in range((used + LANES - 1) // LANES):
        size = min(LANES, used - c * LANES)
        block = xy[pl.ds(c * LANES, LANES), :]
        if size < LANES:
            block = jnp.where(iota((LANES, LANES), 0) < size, block, 0.0)
        zt[...] = block.T
        rows = jnp.concatenate(
            [zt[pl.ds(2 * z, blk, stride=BS), :] + zt[pl.ds(2 * z + 1, blk, stride=BS), :] for z in range(8)],
            axis=0,
        )
        wide = dot(jnp.concatenate(parts_of(rows, 3), axis=0).astype(BF16), interleave, ((1,), (0,)))
        wide = wide[:64] + wide[64:128] + wide[128:]
        for g in range(size // 16):
            tile = wide[0:8, g * LANES:(g + 1) * LANES]
            for z in range(1, 8):
                tile = jnp.where(lane8 == z, wide[z * 8:z * 8 + 8, g * LANES:(g + 1) * LANES], tile)
            rstage[pl.ds(c * 8 + g, count, stride=rchunks), :] = dot(sel, stacked(tile), ((1,), (0,)))
    back = exchange(2, rstage, rrecv, 2 * rchunks)
    for copy in back:
        copy.wait_recv()
    sel = beside(sel_st, count)
    for c in range(rchunks):
        rows = rrecv[pl.ds(c, count, stride=rchunks), :]
        coarse[0, :, pl.ds(c * LANES, LANES)] = dot(sel, stacked(rows), ((1,), (0,)))
    for copy in now_copies + mid_copies + back:
        copy.wait_send()
    result.wait()


def place(out, coarse, out_new, coarse_new, sem):
    copies = [pltpu.make_async_copy(coarse, coarse_new, sem.at[10])]
    half = out.shape[1] // 2
    for f in range(5):
        for k in range(2):
            rows = pl.ds(k * half, half)
            copies.append(pltpu.make_async_copy(out.at[f, rows], out_new.at[f, rows], sem.at[f * 2 + k]))
    for copy in copies:
        copy.start()
    for copy in copies:
        copy.wait()


def shards(n, fine, shell, parent, link):
    group = n[1] * n[2]
    count = 2 * group
    rwidth = 5 * (BS // 2) ** 3
    fine2 = fine.reshape(5, BS * BS, LANES)
    vmem = pl.BlockSpec(memory_space=pltpu.VMEM)
    out, coarse = pl.pallas_call(
        functools.partial(kernel, n),
        out_shape=(
            jax.ShapeDtypeStruct((5, BS * BS, LANES), F32),
            jax.ShapeDtypeStruct((1, shell.shape[1], rwidth), F32),
        ),
        in_specs=[pl.BlockSpec(memory_space=pltpu.HBM)] * 4,
        out_specs=(pl.BlockSpec(memory_space=pltpu.HBM), vmem),
        scratch_shapes=[
            pltpu.VMEM((5, BS * BS, LANES), F32),
            pltpu.VMEM(shell.shape, F32),
            pltpu.VMEM(parent.shape, jnp.int32),
            pltpu.VMEM(link.shape, jnp.int32),
            pltpu.VMEM((5, BS * BS, LANES), F32),
            pltpu.VMEM((5, BS * BS, LANES), F32),
            pltpu.VMEM((2, 5, BS, LANES), F32),
            pltpu.VMEM((2, BS, LANES), F32),
            pltpu.VMEM((2, 2, 5, BS, LANES), F32),
            pltpu.VMEM((2, 2, 5, BS, LANES), F32),
            pltpu.VMEM((2, 2, 2, BS, LANES), F32),
            pltpu.VMEM((2, count * 16, LANES), F32),
            pltpu.VMEM((2, count * 16, LANES), F32),
            pltpu.VMEM((count * (rwidth // LANES), LANES), F32),
            pltpu.VMEM((count * (rwidth // LANES), LANES), F32),
            pltpu.VMEM((1920, LANES), F32),
            pltpu.VMEM((20 * BS, LANES), F32),
            pltpu.VMEM((10 * BS, LANES), F32),
            pltpu.VMEM((10, BS, LANES), F32),
            pltpu.VMEM((384, LANES), F32),
            pltpu.VMEM((LANES, LANES), F32),
            pltpu.SemaphoreType.DMA((9,)),
            pltpu.SemaphoreType.DMA((2, 6)),
            pltpu.SemaphoreType.DMA((2, 6)),
            pltpu.SemaphoreType.DMA((3, group)),
            pltpu.SemaphoreType.DMA((3, group)),
        ],
        compiler_params=pltpu.CompilerParams(
            collective_id=0, has_side_effects=True, vmem_limit_bytes=62 * 1024 * 1024
        ),
    )(fine2, shell, parent, link)
    hbm = pl.BlockSpec(memory_space=pltpu.HBM)
    out, coarse = pl.pallas_call(
        place,
        out_shape=(jax.ShapeDtypeStruct(out.shape, F32), jax.ShapeDtypeStruct(coarse.shape, F32)),
        in_specs=[hbm, hbm],
        out_specs=(hbm, hbm),
        scratch_shapes=[pltpu.SemaphoreType.DMA((11,))],
        compiler_params=pltpu.CompilerParams(vmem_limit_bytes=62 * 1024 * 1024),
    )(out, coarse)
    return out.reshape(fine.shape), coarse


def solution(mesh):
    n = (mesh.shape["gx"], mesh.shape["gy"], mesh.shape["gz"])
    return jax.shard_map(
        functools.partial(shards, n),
        mesh=mesh,
        in_specs=(
            P(None, "gx", "gy", "gz"),
            P("gx", ("gy", "gz"), None),
            P("gx", None),
            P(None, "gx", "gy", "gz"),
        ),
        out_specs=(P(None, "gx", "gy", "gz"), P("gx", ("gy", "gz"), None)),
        check_vma=False,
    )
```

```python
import functools

import jax
import jax.numpy as jnp
from jax import lax
from jax.experimental import pallas as pl
from jax.experimental.pallas import tpu as pltpu
from jax.sharding import PartitionSpec as P

BS = 16
GAMMA = 1.4
LAMBDA = 0.05
LANES = 128
MESH = pl.DeviceIdType.MESH
F32 = jnp.float32
BF16 = jnp.bfloat16


def iota(shape, dim):
    return lax.broadcasted_iota(jnp.int32, shape, dim)


def parts_of(x, count):
    result = []
    for _ in range(count - 1):
        head = x.astype(BF16).astype(F32)
        result.append(head)
        x = x - head
    result.append(x)
    return result


def dot(a, b, contract):
    return lax.dot_general(a, b, (contract, ((), ())), preferred_element_type=F32)


def stacked(x):
    pieces = parts_of(x, 3)
    if x.shape[0] % 16:
        pieces.append(jnp.zeros_like(x))
    return jnp.concatenate(pieces, axis=0).astype(BF16)


def beside(x, rows):
    count = 4 if rows % 16 else 3
    return jnp.concatenate([x] * count, axis=1).astype(BF16)


def prim(u):
    inv = 1.0 / u[0]
    vel = [u[1] * inv, u[2] * inv, u[3] * inv]
    press = (GAMMA - 1.0) * (u[4] - 0.5 * (u[1] * vel[0] + u[2] * vel[1] + u[3] * vel[2]))
    sound = jnp.sqrt(GAMMA * press * inv)
    return vel, press, sound


def flux(u, pr, d):
    vel, press, sound = pr
    vd = vel[d]
    f = [u[1 + d], u[1] * vd, u[2] * vd, u[3] * vd, (u[4] + press) * vd]
    f[1 + d] = f[1 + d] + press
    return f, jnp.abs(vd) + sound


def interface(ul, fl, sl, ur, fr, sr, sign=None):
    wave = jnp.maximum(sl, sr)
    if sign is not None:
        wave = sign * wave
    return [(fl[i] + fr[i]) - wave * (ur[i] - ul[i]) for i in range(5)]


def kernel(
    n,
    fine, shell_hbm, parent_hbm, link_hbm, out_hbm, coarse,
    out, shell, parent, link, s0, s1, ypack, zpack, hx, hy, hz, sstage, srecv, rstage, rrecv, rstage2, rrecv2, xt, cxy, cz, cells_z, xy, zt,
    load_sem, halo_send, halo_recv, all_send, all_recv,
):
    nx, ny, nz = n
    group = ny * nz
    count = 2 * group
    gx, gy, gz = lax.axis_index("gx"), lax.axis_index("gy"), lax.axis_index("gz")
    me = gy * nz + gz
    blk = shell.shape[1]
    width = shell.shape[2] // 2
    chunks = width // LANES
    rwidth = coarse.shape[2]
    rchunks = rwidth // LANES
    nq = parent.shape[1]
    peers = []
    for i in range(1, group):
        peer = lax.rem(me + i, group)
        peers.append((gx, peer // nz, lax.rem(peer, nz)))
    xlo, xhi = (lax.rem(gx + nx - 1, nx), gy, gz), (lax.rem(gx + 1, nx), gy, gz)
    ylo, yhi = (gx, lax.rem(gy + ny - 1, ny), gz), (gx, lax.rem(gy + 1, ny), gz)
    zlo, zhi = (gx, gy, lax.rem(gz + nz - 1, nz)), (gx, gy, lax.rem(gz + 1, nz))

    barrier = pltpu.get_barrier_semaphore()
    greeted = peers + [xlo, xhi]
    for dev in greeted:
        pl.semaphore_signal(barrier, inc=1, device_id=dev, device_id_type=MESH)

    loads = []
    for k, (src, dst) in enumerate(((parent_hbm, parent), (shell_hbm, shell), (link_hbm, link))):
        load = pltpu.make_async_copy(src, dst, load_sem.at[5 + k])
        load.start()
        loads.append(load)
    for f in range(5):
        load = pltpu.make_async_copy(fine.at[f], s0.at[f], load_sem.at[f])
        load.start()
        loads.append(load)

    loads[0].wait()
    par = parent[...]
    lane_q = iota((1, nq), 1)
    owner = par // blk
    rank = jnp.zeros((1, nq), jnp.int32)
    for j in range(1, blk):
        before = pltpu.roll(jnp.broadcast_to(owner, (8, nq)), j, 1)[0:1]
        rank = rank + jnp.where((lane_q % blk >= j) & (before == owner), 1, 0)
    at_owner = (lane_q // blk) * 2 + rank
    at_block = owner * 2 + rank
    to_t = (jnp.broadcast_to(at_owner, (count, nq)) == iota((count, nq), 0)).astype(F32).astype(BF16)
    mine = (jnp.broadcast_to(par, (blk, nq)) == me * blk + iota((blk, nq), 0)).astype(F32).astype(BF16)
    sel_ts = dot(to_t, mine, ((1,), (1,)))
    sel_st = dot(mine, to_t, ((1,), (1,)))
    at_block8 = jnp.broadcast_to(at_block.astype(F32), (8, nq)).astype(BF16)
    spread = (iota((nq, LANES), 0) == me * blk + iota((nq, LANES), 1) // BS).astype(F32).astype(BF16)
    pick = (iota((nq, blk), 0) == me * blk + iota((nq, blk), 1)).astype(F32).astype(BF16)
    row_lane = dot(at_block8, spread, ((1,), (0,)))[0:1]
    block_hi = ((iota((nq, LANES), 1) + 1) // BS + blk - 1) % blk
    spread_hi = (iota((nq, LANES), 0) == me * blk + block_hi).astype(F32).astype(BF16)
    row_lane_hi = dot(at_block8, spread_hi, ((1,), (0,)))[0:1]
    row_blk = dot(at_block8, pick, ((1,), (0,)))[0:1]
    be = (jnp.broadcast_to(row_lane, (count, LANES)) == iota((count, LANES), 0).astype(F32)).astype(F32)
    be3 = jnp.concatenate([be] * 3, axis=0).astype(BF16)
    be_hi = (jnp.broadcast_to(row_lane_hi, (count, LANES)) == iota((count, LANES), 0).astype(F32)).astype(F32)
    be3_hi = jnp.concatenate([be_hi] * 3, axis=0).astype(BF16)
    sel_tk = (jnp.broadcast_to(row_blk, (count, blk)) == iota((count, blk), 0).astype(F32)).astype(F32)

    loads[1].wait()
    sel = beside(sel_ts, blk)
    for c in range(chunks):
        now = shell[0, :, pl.ds(c * LANES, LANES)]
        end = shell[0, :, pl.ds(width + c * LANES, LANES)]
        both = jnp.concatenate([stacked(now), stacked(0.5 * (now + end))], axis=1)
        rows = dot(sel, both, ((1,), (0,)))
        sstage[0, pl.ds(c, count, stride=16), :] = rows[:, :LANES]
        sstage[1, pl.ds(c, count, stride=16), :] = rows[:, LANES:]

    lane = iota((BS, LANES), 1)
    sub = iota((BS, LANES), 0)
    even = lane % 2 == 0
    pair = ((lane + 1) // 2) % 8
    first_pairs = (lane + 1) % LANES < 16

    def plane(ref, f, x):
        return ref[f, pl.ds(x * BS, BS), :]

    def pack_y(ref):
        for f in range(5):
            ypack[0, f] = ref[f, pl.ds(0, BS, stride=BS), :]
            ypack[1, f] = ref[f, pl.ds(BS - 1, BS, stride=BS), :]

    def pack_z(ref):
        packed = [jnp.zeros((BS, LANES), F32)] * 2
        for f in range(5):
            for g in range(2):
                tile = plane(ref, f, 8 * g)
                for x in range(1, 8):
                    tile = jnp.where(pair == x, pltpu.roll(plane(ref, f, 8 * g + x), 2 * x, 1), tile)
                k = f * 2 + g
                cells_z[k] = tile
                moved = tile if k % 8 == 0 else pltpu.roll(tile, 16 * (k % 8), 1)
                packed[k // 8] = jnp.where(((lane + 1) // 16) % 8 == k % 8, moved, packed[k // 8])
        zpack[0] = packed[0]
        zpack[1] = packed[1]

    def halos(ref, step):
        def send(k, src, dst, dev):
            copy = pltpu.make_async_remote_copy(
                src_ref=src, dst_ref=dst, send_sem=halo_send.at[step, k], recv_sem=halo_recv.at[step, k],
                device_id=dev, device_id_type=MESH,
            )
            copy.start()
            return copy

        return [
            send(0, ref.at[:, pl.ds(BS * BS - BS, BS)], hx.at[step, 0], xhi),
            send(1, ref.at[:, pl.ds(0, BS)], hx.at[step, 1], xlo),
            send(2, ypack.at[1], hy.at[step, 0], yhi),
            send(3, ypack.at[0], hy.at[step, 1], ylo),
            send(4, zpack, hz.at[step, 0], zhi),
            send(5, zpack, hz.at[step, 1], zlo),
        ]

    def exchange(kind, stage, recv, rows):
        copies = []
        for i, dev in enumerate(peers):
            to = lax.rem(me + i + 1, group)
            copy = pltpu.make_async_remote_copy(
                src_ref=stage.at[pl.ds(pl.multiple_of(to * rows, 8), rows)],
                dst_ref=recv.at[pl.ds(pl.multiple_of(me * rows, 8), rows)],
                send_sem=all_send.at[kind, i], recv_sem=all_recv.at[kind, i],
                device_id=dev, device_id_type=MESH,
            )
            copy.start()
            copies.append(copy)
        own = pl.ds(pl.multiple_of(me * rows, 8), rows)
        recv[own, :] = stage[own, :]
        return copies

    for load in loads[2:]:
        load.wait()
    pl.semaphore_wait(barrier, len(greeted))
    now_copies = exchange(0, sstage.at[0], srecv.at[0], 32)
    pack_y(s0)
    pack_z(s0)
    halo0 = halos(s0, 0)
    mid_copies = exchange(1, sstage.at[1], srecv.at[1], 32)

    linkf = jnp.concatenate([link[k, 0] for k in range(6)] + [jnp.zeros((2, blk), jnp.int32)], axis=0)
    over = (iota((blk, LANES), 0) == iota((blk, LANES), 1) // BS).astype(F32).astype(BF16)
    over_hi = (iota((blk, LANES), 0) == ((iota((blk, LANES), 1) + 1) // BS + blk - 1) % blk).astype(F32).astype(BF16)
    linkb = linkf.astype(F32).astype(BF16)
    mask = dot(linkb, over, ((1,), (0,)))
    mask_hi = dot(linkb, over_hi, ((1,), (0,)))
    is_lo = lane % BS == 0
    at_end = is_lo | (lane % BS == BS - 1)
    zmask = jnp.where(even, mask[4:5], mask_hi[5:6]) > 0.5
    half_lane = (iota((8, LANES), 1) % BS) // 2
    even8 = iota((8, LANES), 1) % 2 == 0
    pair8 = (((iota((8, LANES), 1) + 1) // 2) % 8) // 2

    def expand(level):
        for c in range(chunks):
            rows = stacked(srecv[level, pl.ds(c, count, stride=16), :])
            if c * LANES < 1600:
                xt[pl.ds(c * LANES, LANES), :] = dot(rows, be3, ((0,), (0,)))
            if (c + 1) * LANES > 1600:
                skip = max(0, 1600 - c * LANES)
                xt[pl.ds(c * LANES + skip, LANES - skip), :] = dot(rows, be3_hi, ((0,), (0,)))[skip:]
        for k in range(20):
            tile = xt[pl.ds(k * 64, 8, stride=8), :]
            for b in range(1, 8):
                tile = jnp.where(half_lane == b, xt[pl.ds(k * 64 + b, 8, stride=8), :], tile)
            cxy[pl.ds(k * BS, 8, stride=2), :] = tile
            cxy[pl.ds(k * BS + 1, 8, stride=2), :] = tile
        for k in range(10):
            tile = None
            for a in range(4):
                at = ((k // 2) * 8 + 4 * (k % 2) + a) * 8
                piece = jnp.where(even8, xt[pl.ds(1280 + at, 8), :], xt[pl.ds(1600 + at, 8), :])
                tile = piece if a == 0 else jnp.where(pair8 == a, piece, tile)
            cz[pl.ds(k * BS, 8, stride=2), :] = tile
            cz[pl.ds(k * BS + 1, 8, stride=2), :] = tile

    def inner(ref, dst):
        def step_x(x, hxl, u, pr, last):
            if last:
                total = [-hxl[f] for f in range(5)]
                hxr, un, prn = hxl, u, pr
            else:
                at = pl.multiple_of((x + 1) * BS, BS)
                un = [ref[f, pl.ds(at, BS), :] for f in range(5)]
                prn = prim(un)
                fc, sc = flux(u, pr, 0)
                fn, sn = flux(un, prn, 0)
                hxr = interface(u, fc, sc, un, fn, sn)
                total = [hxr[f] - hxl[f] for f in range(5)]
            for d, axis, edge in ((1, 0, sub == 0), (2, 1, is_lo)):
                fc, sc = flux(u, pr, d)
                ub = [pltpu.roll(a, 1, axis) for a in u]
                fb = [pltpu.roll(a, 1, axis) for a in fc]
                low = interface(ub, fb, pltpu.roll(sc, 1, axis), u, fc, sc)
                for f in range(5):
                    lo = jnp.where(edge, 0.0, low[f])
                    total[f] = total[f] + (pltpu.roll(lo, lo.shape[axis] - 1, axis) - lo)
            at = pl.multiple_of(x * BS, BS)
            for f in range(5):
                dst[f, pl.ds(at, BS), :] = u[f] - (0.5 * LAMBDA) * total[f]
            return hxr, un, prn

        u = [plane(ref, f, 0) for f in range(5)]
        zero = [jnp.zeros((BS, LANES), F32)] * 5
        carry = lax.fori_loop(
            0, BS - 1, lambda x, carry: step_x(x, *carry, False), (zero, u, prim(u)), unroll=3
        )
        step_x(BS - 1, *carry, True)

    def faces(ghost, cells, d, sign):
        gf, gs = flux(ghost, prim(ghost), d)
        cf, cs = flux(cells, prim(cells), d)
        return interface(ghost, gf, gs, cells, cf, cs, sign)

    def outer(ref, dst, step):
        for d in range(2):
            for side in range(2):
                chosen = jnp.broadcast_to(mask[2 * d + side:2 * d + side + 1], (BS, LANES)) > 0.5
                halo = hx if d == 0 else hy
                if d == 0:
                    rows = pl.ds(side * (BS - 1) * BS, BS)
                else:
                    rows = pl.ds(side * (BS - 1), BS, stride=BS)
                ghost = [
                    jnp.where(chosen, halo[step, side, f], cxy[pl.ds(((2 * d + side) * 5 + f) * BS, BS), :])
                    for f in range(5)
                ]
                cells = [ref[f, rows, :] for f in range(5)]
                face = faces(ghost, cells, d, 1.0 - 2 * side)
                for f in range(5):
                    dst[f, rows, :] = dst[f, rows, :] + (0.5 - side) * LAMBDA * face[f]
        comb = []
        for k in range(2):
            left = pltpu.roll(hz[step, 0, k], 1, 1)
            right = pltpu.roll(hz[step, 1, k], LANES - 1, 1)
            comb.append(jnp.where(even, left, right))
        sign = jnp.where(even, 1.0, -1.0)
        scale = (0.5 * LAMBDA) * sign
        for g in range(2):
            cells, ghost = [], []
            for f in range(5):
                k = f * 2 + g
                tile = cells_z[k]
                near = jnp.where(even, pltpu.roll(tile, 1, 1), pltpu.roll(tile, LANES - 1, 1))
                far = comb[k // 8]
                if k % 8:
                    far = pltpu.roll(far, LANES - 16 * (k % 8), 1)
                fine_side = jnp.where(first_pairs, far, near)
                cells.append(tile)
                ghost.append(jnp.where(zmask, fine_side, cz[pl.ds(k * BS, BS), :]))
            face = faces(ghost, cells, 2, sign)
            for f in range(5):
                change = scale * face[f]
                for x in range(8):
                    moved = change if x == 0 else pltpu.roll(change, LANES - 2 * x, 1)
                    rows = pl.ds((8 * g + x) * BS, BS)
                    dst[f, rows, :] = dst[f, rows, :] + jnp.where(at_end, moved, 0.0)

    inner(s0, s1)
    for copy in now_copies:
        copy.wait_recv()
    expand(0)
    for copy in halo0:
        copy.wait()
    outer(s0, s1, 0)
    pack_y(s1)
    pack_z(s1)
    halo1 = halos(s1, 1)
    for copy in mid_copies:
        copy.wait_recv()
    expand(1)
    inner(s1, out)
    for copy in halo1:
        copy.wait()
    outer(s1, out, 1)
    result = pltpu.make_async_copy(out, out_hbm, load_sem.at[8])
    result.start()

    for f in range(5):
        for a in range(8):
            total = None
            for x in range(2):
                for y in range(2):
                    piece = out[f, pl.ds((2 * a + x) * BS + y, 8, stride=2), :]
                    total = piece if total is None else total + piece
            xy[pl.ds((f * 8 + a) * 8, 8), :] = 0.125 * total
    used = 5 * 64
    interleave = (iota((LANES, 8 * LANES), 0) == iota((LANES, 8 * LANES), 1) // 8).astype(F32).astype(BF16)
    lane8 = iota((blk, LANES), 1) % 8
    sel = beside(sel_tk, blk)
    back = []
    for c in range((used + LANES - 1) // LANES):
        size = min(LANES, used - c * LANES)
        block = xy[pl.ds(c * LANES, LANES), :]
        if size < LANES:
            block = jnp.where(iota((LANES, LANES), 0) < size, block, 0.0)
        zt[...] = block.T
        rows = jnp.concatenate(
            [zt[pl.ds(2 * z, blk, stride=BS), :] + zt[pl.ds(2 * z + 1, blk, stride=BS), :] for z in range(8)],
            axis=0,
        )
        wide = dot(jnp.concatenate(parts_of(rows, 3), axis=0).astype(BF16), interleave, ((1,), (0,)))
        wide = wide[:64] + wide[64:128] + wide[128:]
        tiles = []
        for g in range(size // 16):
            tile = wide[0:8, g * LANES:(g + 1) * LANES]
            for z in range(1, 8):
                tile = jnp.where(lane8 == z, wide[z * 8:z * 8 + 8, g * LANES:(g + 1) * LANES], tile)
            tiles.append(tile)
        routed = dot(sel, stacked(jnp.concatenate(tiles, axis=1)), ((1,), (0,)))
        stage, first, each = (rstage, 0, 8) if c == 0 else (rstage2, (c - 1) * 8, rchunks - 8)
        for g in range(size // 16):
            stage[pl.ds(first + g, count, stride=each), :] = routed[:, g * LANES:(g + 1) * LANES]
        if c == 0:
            back.append(exchange(2, rstage, rrecv, 2 * 8))
    back.append(exchange(3, rstage2, rrecv2, 2 * (rchunks - 8)))
    sel = beside(sel_st, count)
    for half, (recv, first, each) in enumerate(((rrecv, 0, 8), (rrecv2, 8, rchunks - 8))):
        for copy in back[half]:
            copy.wait_recv()
        for c in range(each):
            rows = recv[pl.ds(c, count, stride=each), :]
            coarse[0, :, pl.ds((first + c) * LANES, LANES)] = dot(sel, stacked(rows), ((1,), (0,)))
    for copy in now_copies + mid_copies + back[0] + back[1]:
        copy.wait_send()
    result.wait()


def place(out, coarse, out_new, coarse_new, held, held_coarse, sem):
    steps = [(coarse, held_coarse, coarse_new)]
    steps += [(out.at[f], held.at[f], out_new.at[f]) for f in range(5)]
    loads = [pltpu.make_async_copy(src, mid, sem.at[0, k]) for k, (src, mid, _) in enumerate(steps)]
    stores = [pltpu.make_async_copy(mid, dst, sem.at[1, k]) for k, (_, mid, dst) in enumerate(steps)]
    for copy in loads:
        copy.start()
    for load, copy in zip(loads, stores):
        load.wait()
        copy.start()
    for copy in stores:
        copy.wait()


def shards(n, fine, shell, parent, link):
    group = n[1] * n[2]
    count = 2 * group
    rwidth = 5 * (BS // 2) ** 3
    fine2 = fine.reshape(5, BS * BS, LANES)
    vmem = pl.BlockSpec(memory_space=pltpu.VMEM)
    out, coarse = pl.pallas_call(
        functools.partial(kernel, n),
        out_shape=(
            jax.ShapeDtypeStruct((5, BS * BS, LANES), F32),
            jax.ShapeDtypeStruct((1, shell.shape[1], rwidth), F32),
        ),
        in_specs=[pl.BlockSpec(memory_space=pltpu.HBM)] * 4,
        out_specs=(pl.BlockSpec(memory_space=pltpu.HBM), vmem),
        scratch_shapes=[
            pltpu.VMEM((5, BS * BS, LANES), F32),
            pltpu.VMEM(shell.shape, F32),
            pltpu.VMEM(parent.shape, jnp.int32),
            pltpu.VMEM(link.shape, jnp.int32),
            pltpu.VMEM((5, BS * BS, LANES), F32),
            pltpu.VMEM((5, BS * BS, LANES), F32),
            pltpu.VMEM((2, 5, BS, LANES), F32),
            pltpu.VMEM((2, BS, LANES), F32),
            pltpu.VMEM((2, 2, 5, BS, LANES), F32),
            pltpu.VMEM((2, 2, 5, BS, LANES), F32),
            pltpu.VMEM((2, 2, 2, BS, LANES), F32),
            pltpu.VMEM((2, count * 16, LANES), F32),
            pltpu.VMEM((2, count * 16, LANES), F32),
            pltpu.VMEM((count * 8, LANES), F32),
            pltpu.VMEM((count * 8, LANES), F32),
            pltpu.VMEM((count * (rwidth // LANES - 8), LANES), F32),
            pltpu.VMEM((count * (rwidth // LANES - 8), LANES), F32),
            pltpu.VMEM((1920, LANES), F32),
            pltpu.VMEM((20 * BS, LANES), F32),
            pltpu.VMEM((10 * BS, LANES), F32),
            pltpu.VMEM((10, BS, LANES), F32),
            pltpu.VMEM((384, LANES), F32),
            pltpu.VMEM((LANES, LANES), F32),
            pltpu.SemaphoreType.DMA((9,)),
            pltpu.SemaphoreType.DMA((2, 6)),
            pltpu.SemaphoreType.DMA((2, 6)),
            pltpu.SemaphoreType.DMA((4, group)),
            pltpu.SemaphoreType.DMA((4, group)),
        ],
        compiler_params=pltpu.CompilerParams(
            collective_id=0, has_side_effects=True, vmem_limit_bytes=62 * 1024 * 1024
        ),
    )(fine2, shell, parent, link)
    hbm = pl.BlockSpec(memory_space=pltpu.HBM)
    out, coarse = pl.pallas_call(
        place,
        out_shape=(jax.ShapeDtypeStruct(out.shape, F32), jax.ShapeDtypeStruct(coarse.shape, F32)),
        in_specs=[hbm, hbm],
        out_specs=(hbm, hbm),
        scratch_shapes=[
            pltpu.VMEM(out.shape, F32),
            pltpu.VMEM(coarse.shape, F32),
            pltpu.SemaphoreType.DMA((2, 6)),
        ],
        compiler_params=pltpu.CompilerParams(vmem_limit_bytes=62 * 1024 * 1024),
    )(out, coarse)
    return out.reshape(fine.shape), coarse


def solution(mesh):
    n = (mesh.shape["gx"], mesh.shape["gy"], mesh.shape["gz"])
    return jax.shard_map(
        functools.partial(shards, n),
        mesh=mesh,
        in_specs=(
            P(None, "gx", "gy", "gz"),
            P("gx", ("gy", "gz"), None),
            P("gx", None),
            P(None, "gx", "gy", "gz"),
        ),
        out_specs=(P(None, "gx", "gy", "gz"), P("gx", ("gy", "gz"), None)),
        check_vma=False,
    )
```

```python
import functools

import jax
import jax.numpy as jnp
from jax import lax
from jax.experimental import pallas as pl
from jax.experimental.pallas import tpu as pltpu
from jax.sharding import PartitionSpec as P

BS = 16
GAMMA = 1.4
LAMBDA = 0.05
LANES = 128
MESH = pl.DeviceIdType.MESH
F32 = jnp.float32
BF16 = jnp.bfloat16


def iota(shape, dim):
    return lax.broadcasted_iota(jnp.int32, shape, dim)


def parts_of(x, count):
    result = []
    for _ in range(count - 1):
        head = x.astype(BF16).astype(F32)
        result.append(head)
        x = x - head
    result.append(x)
    return result


def dot(a, b, contract):
    return lax.dot_general(a, b, (contract, ((), ())), preferred_element_type=F32)


def stacked(x):
    pieces = parts_of(x, 3)
    if x.shape[0] % 16:
        pieces.append(jnp.zeros_like(x))
    return jnp.concatenate(pieces, axis=0).astype(BF16)


def beside(x, rows):
    count = 4 if rows % 16 else 3
    return jnp.concatenate([x] * count, axis=1).astype(BF16)


def prim(u):
    inv = 1.0 / u[0]
    vel = [u[1] * inv, u[2] * inv, u[3] * inv]
    press = (GAMMA - 1.0) * (u[4] - 0.5 * (u[1] * vel[0] + u[2] * vel[1] + u[3] * vel[2]))
    sound = jnp.sqrt(GAMMA * press * inv)
    return vel, press, sound


def flux(u, pr, d):
    vel, press, sound = pr
    vd = vel[d]
    f = [u[1 + d], u[1] * vd, u[2] * vd, u[3] * vd, (u[4] + press) * vd]
    f[1 + d] = f[1 + d] + press
    return f, jnp.abs(vd) + sound


def interface(ul, fl, sl, ur, fr, sr, sign=None):
    wave = jnp.maximum(sl, sr)
    if sign is not None:
        wave = sign * wave
    return [(fl[i] + fr[i]) - wave * (ur[i] - ul[i]) for i in range(5)]


def kernel(
    n,
    fine, shell_hbm, parent_hbm, link_hbm, out, coarse,
    shell, parent, link, s0, s1, ypack, zpack, hx, hy, hz, sstage, srecv, rstage, rrecv, rstage2, rrecv2, xt, cxy, cz, cells_z, xy, zt,
    load_sem, halo_send, halo_recv, all_send, all_recv,
):
    nx, ny, nz = n
    group = ny * nz
    count = 2 * group
    gx, gy, gz = lax.axis_index("gx"), lax.axis_index("gy"), lax.axis_index("gz")
    me = gy * nz + gz
    blk = shell.shape[1]
    width = shell.shape[2] // 2
    chunks = width // LANES
    rwidth = coarse.shape[2]
    rchunks = rwidth // LANES
    nq = parent.shape[1]
    peers = []
    for i in range(1, group):
        peer = lax.rem(me + i, group)
        peers.append((gx, peer // nz, lax.rem(peer, nz)))
    xlo, xhi = (lax.rem(gx + nx - 1, nx), gy, gz), (lax.rem(gx + 1, nx), gy, gz)
    ylo, yhi = (gx, lax.rem(gy + ny - 1, ny), gz), (gx, lax.rem(gy + 1, ny), gz)
    zlo, zhi = (gx, gy, lax.rem(gz + nz - 1, nz)), (gx, gy, lax.rem(gz + 1, nz))

    barrier = pltpu.get_barrier_semaphore()
    greeted = peers + [xlo, xhi]
    for dev in greeted:
        pl.semaphore_signal(barrier, inc=1, device_id=dev, device_id_type=MESH)

    loads = []
    for k, (src, dst) in enumerate(((parent_hbm, parent), (shell_hbm, shell), (link_hbm, link))):
        load = pltpu.make_async_copy(src, dst, load_sem.at[5 + k])
        load.start()
        loads.append(load)
    for f in range(5):
        load = pltpu.make_async_copy(fine.at[f], s0.at[f], load_sem.at[f])
        load.start()
        loads.append(load)

    loads[0].wait()
    par = parent[...]
    lane_q = iota((1, nq), 1)
    owner = par // blk
    rank = jnp.zeros((1, nq), jnp.int32)
    for j in range(1, blk):
        before = pltpu.roll(jnp.broadcast_to(owner, (8, nq)), j, 1)[0:1]
        rank = rank + jnp.where((lane_q % blk >= j) & (before == owner), 1, 0)
    at_owner = (lane_q // blk) * 2 + rank
    at_block = owner * 2 + rank
    to_t = (jnp.broadcast_to(at_owner, (count, nq)) == iota((count, nq), 0)).astype(F32).astype(BF16)
    mine = (jnp.broadcast_to(par, (blk, nq)) == me * blk + iota((blk, nq), 0)).astype(F32).astype(BF16)
    sel_ts = dot(to_t, mine, ((1,), (1,)))
    sel_st = dot(mine, to_t, ((1,), (1,)))
    at_block8 = jnp.broadcast_to(at_block.astype(F32), (8, nq)).astype(BF16)
    spread = (iota((nq, LANES), 0) == me * blk + iota((nq, LANES), 1) // BS).astype(F32).astype(BF16)
    pick = (iota((nq, blk), 0) == me * blk + iota((nq, blk), 1)).astype(F32).astype(BF16)
    row_lane = dot(at_block8, spread, ((1,), (0,)))[0:1]
    block_hi = ((iota((nq, LANES), 1) + 1) // BS + blk - 1) % blk
    spread_hi = (iota((nq, LANES), 0) == me * blk + block_hi).astype(F32).astype(BF16)
    row_lane_hi = dot(at_block8, spread_hi, ((1,), (0,)))[0:1]
    row_blk = dot(at_block8, pick, ((1,), (0,)))[0:1]
    be = (jnp.broadcast_to(row_lane, (count, LANES)) == iota((count, LANES), 0).astype(F32)).astype(F32)
    be3 = jnp.concatenate([be] * 3, axis=0).astype(BF16)
    be_hi = (jnp.broadcast_to(row_lane_hi, (count, LANES)) == iota((count, LANES), 0).astype(F32)).astype(F32)
    be3_hi = jnp.concatenate([be_hi] * 3, axis=0).astype(BF16)
    sel_tk = (jnp.broadcast_to(row_blk, (count, blk)) == iota((count, blk), 0).astype(F32)).astype(F32)

    loads[1].wait()
    sel = beside(sel_ts, blk)

    def stage_level(level):
        for c in range(chunks):
            value = shell[0, :, pl.ds(c * LANES, LANES)]
            if level:
                value = 0.5 * (value + shell[0, :, pl.ds(width + c * LANES, LANES)])
            sstage[level, pl.ds(c, count, stride=16), :] = dot(sel, stacked(value), ((1,), (0,)))

    stage_level(0)

    lane = iota((BS, LANES), 1)
    sub = iota((BS, LANES), 0)
    even = lane % 2 == 0
    pair = ((lane + 1) // 2) % 8
    first_pairs = (lane + 1) % LANES < 16

    def plane(ref, f, x):
        return ref[f, pl.ds(x * BS, BS), :]

    def pack_y(ref):
        for f in range(5):
            ypack[0, f] = ref[f, pl.ds(0, BS, stride=BS), :]
            ypack[1, f] = ref[f, pl.ds(BS - 1, BS, stride=BS), :]

    def pack_z(ref):
        packed = [jnp.zeros((BS, LANES), F32)] * 2
        for f in range(5):
            for g in range(2):
                tile = plane(ref, f, 8 * g)
                for x in range(1, 8):
                    tile = jnp.where(pair == x, pltpu.roll(plane(ref, f, 8 * g + x), 2 * x, 1), tile)
                k = f * 2 + g
                cells_z[k] = tile
                moved = tile if k % 8 == 0 else pltpu.roll(tile, 16 * (k % 8), 1)
                packed[k // 8] = jnp.where(((lane + 1) // 16) % 8 == k % 8, moved, packed[k // 8])
        zpack[0] = packed[0]
        zpack[1] = packed[1]

    def halos(ref, step):
        def send(k, src, dst, dev):
            copy = pltpu.make_async_remote_copy(
                src_ref=src, dst_ref=dst, send_sem=halo_send.at[step, k], recv_sem=halo_recv.at[step, k],
                device_id=dev, device_id_type=MESH,
            )
            copy.start()
            return copy

        return [
            send(0, ref.at[:, pl.ds(BS * BS - BS, BS)], hx.at[step, 0], xhi),
            send(1, ref.at[:, pl.ds(0, BS)], hx.at[step, 1], xlo),
            send(2, ypack.at[1], hy.at[step, 0], yhi),
            send(3, ypack.at[0], hy.at[step, 1], ylo),
            send(4, zpack, hz.at[step, 0], zhi),
            send(5, zpack, hz.at[step, 1], zlo),
        ]

    def exchange(kind, stage, recv, rows):
        copies = []
        for i, dev in enumerate(peers):
            to = lax.rem(me + i + 1, group)
            copy = pltpu.make_async_remote_copy(
                src_ref=stage.at[pl.ds(pl.multiple_of(to * rows, 8), rows)],
                dst_ref=recv.at[pl.ds(pl.multiple_of(me * rows, 8), rows)],
                send_sem=all_send.at[kind, i], recv_sem=all_recv.at[kind, i],
                device_id=dev, device_id_type=MESH,
            )
            copy.start()
            copies.append(copy)
        own = pl.ds(pl.multiple_of(me * rows, 8), rows)
        recv[own, :] = stage[own, :]
        return copies

    for load in loads[2:]:
        load.wait()
    pl.semaphore_wait(barrier, len(greeted))
    now_copies = exchange(0, sstage.at[0], srecv.at[0], 32)
    pack_y(s0)
    pack_z(s0)
    halo0 = halos(s0, 0)

    linkf = jnp.concatenate([link[k, 0] for k in range(6)] + [jnp.zeros((2, blk), jnp.int32)], axis=0)
    over = (iota((blk, LANES), 0) == iota((blk, LANES), 1) // BS).astype(F32).astype(BF16)
    over_hi = (iota((blk, LANES), 0) == ((iota((blk, LANES), 1) + 1) // BS + blk - 1) % blk).astype(F32).astype(BF16)
    linkb = linkf.astype(F32).astype(BF16)
    mask = dot(linkb, over, ((1,), (0,)))
    mask_hi = dot(linkb, over_hi, ((1,), (0,)))
    is_lo = lane % BS == 0
    at_end = is_lo | (lane % BS == BS - 1)
    zmask = jnp.where(even, mask[4:5], mask_hi[5:6]) > 0.5
    half_lane = (iota((8, LANES), 1) % BS) // 2
    even8 = iota((8, LANES), 1) % 2 == 0
    pair8 = (((iota((8, LANES), 1) + 1) // 2) % 8) // 2

    def expand(level):
        for c in range(chunks):
            rows = stacked(srecv[level, pl.ds(c, count, stride=16), :])
            if c * LANES < 1600:
                xt[pl.ds(c * LANES, LANES), :] = dot(rows, be3, ((0,), (0,)))
            if (c + 1) * LANES > 1600:
                skip = max(0, 1600 - c * LANES)
                xt[pl.ds(c * LANES + skip, LANES - skip), :] = dot(rows, be3_hi, ((0,), (0,)))[skip:]
        for k in range(20):
            tile = xt[pl.ds(k * 64, 8, stride=8), :]
            for b in range(1, 8):
                tile = jnp.where(half_lane == b, xt[pl.ds(k * 64 + b, 8, stride=8), :], tile)
            cxy[pl.ds(k * BS, 8, stride=2), :] = tile
            cxy[pl.ds(k * BS + 1, 8, stride=2), :] = tile
        for k in range(10):
            tile = None
            for a in range(4):
                at = ((k // 2) * 8 + 4 * (k % 2) + a) * 8
                piece = jnp.where(even8, xt[pl.ds(1280 + at, 8), :], xt[pl.ds(1600 + at, 8), :])
                tile = piece if a == 0 else jnp.where(pair8 == a, piece, tile)
            cz[pl.ds(k * BS, 8, stride=2), :] = tile
            cz[pl.ds(k * BS + 1, 8, stride=2), :] = tile

    def inner(ref, dst):
        def step_x(x, hxl, u, pr, last):
            if last:
                total = [-hxl[f] for f in range(5)]
                hxr, un, prn = hxl, u, pr
            else:
                at = pl.multiple_of((x + 1) * BS, BS)
                un = [ref[f, pl.ds(at, BS), :] for f in range(5)]
                prn = prim(un)
                fc, sc = flux(u, pr, 0)
                fn, sn = flux(un, prn, 0)
                hxr = interface(u, fc, sc, un, fn, sn)
                total = [hxr[f] - hxl[f] for f in range(5)]
            for d, axis, edge in ((1, 0, sub == 0), (2, 1, is_lo)):
                fc, sc = flux(u, pr, d)
                ub = [pltpu.roll(a, 1, axis) for a in u]
                fb = [pltpu.roll(a, 1, axis) for a in fc]
                low = interface(ub, fb, pltpu.roll(sc, 1, axis), u, fc, sc)
                for f in range(5):
                    lo = jnp.where(edge, 0.0, low[f])
                    total[f] = total[f] + (pltpu.roll(lo, lo.shape[axis] - 1, axis) - lo)
            at = pl.multiple_of(x * BS, BS)
            for f in range(5):
                dst[f, pl.ds(at, BS), :] = u[f] - (0.5 * LAMBDA) * total[f]
            return hxr, un, prn

        u = [plane(ref, f, 0) for f in range(5)]
        zero = [jnp.zeros((BS, LANES), F32)] * 5
        carry = lax.fori_loop(
            0, BS - 1, lambda x, carry: step_x(x, *carry, False), (zero, u, prim(u)), unroll=3
        )
        step_x(BS - 1, *carry, True)

    def faces(ghost, cells, d, sign):
        gf, gs = flux(ghost, prim(ghost), d)
        cf, cs = flux(cells, prim(cells), d)
        return interface(ghost, gf, gs, cells, cf, cs, sign)

    def outer(ref, dst, step):
        for d in range(2):
            for side in range(2):
                chosen = jnp.broadcast_to(mask[2 * d + side:2 * d + side + 1], (BS, LANES)) > 0.5
                halo = hx if d == 0 else hy
                if d == 0:
                    rows = pl.ds(side * (BS - 1) * BS, BS)
                else:
                    rows = pl.ds(side * (BS - 1), BS, stride=BS)
                ghost = [
                    jnp.where(chosen, halo[step, side, f], cxy[pl.ds(((2 * d + side) * 5 + f) * BS, BS), :])
                    for f in range(5)
                ]
                cells = [ref[f, rows, :] for f in range(5)]
                face = faces(ghost, cells, d, 1.0 - 2 * side)
                for f in range(5):
                    dst[f, rows, :] = dst[f, rows, :] + (0.5 - side) * LAMBDA * face[f]
        comb = []
        for k in range(2):
            left = pltpu.roll(hz[step, 0, k], 1, 1)
            right = pltpu.roll(hz[step, 1, k], LANES - 1, 1)
            comb.append(jnp.where(even, left, right))
        sign = jnp.where(even, 1.0, -1.0)
        scale = (0.5 * LAMBDA) * sign
        for g in range(2):
            cells, ghost = [], []
            for f in range(5):
                k = f * 2 + g
                tile = cells_z[k]
                near = jnp.where(even, pltpu.roll(tile, 1, 1), pltpu.roll(tile, LANES - 1, 1))
                far = comb[k // 8]
                if k % 8:
                    far = pltpu.roll(far, LANES - 16 * (k % 8), 1)
                fine_side = jnp.where(first_pairs, far, near)
                cells.append(tile)
                ghost.append(jnp.where(zmask, fine_side, cz[pl.ds(k * BS, BS), :]))
            face = faces(ghost, cells, 2, sign)
            for f in range(5):
                change = scale * face[f]
                for x in range(8):
                    moved = change if x == 0 else pltpu.roll(change, LANES - 2 * x, 1)
                    rows = pl.ds((8 * g + x) * BS, BS)
                    dst[f, rows, :] = dst[f, rows, :] + jnp.where(at_end, moved, 0.0)

    inner(s0, s1)
    stage_level(1)
    mid_copies = exchange(1, sstage.at[1], srecv.at[1], 32)
    for copy in now_copies:
        copy.wait_recv()
    expand(0)
    for copy in halo0:
        copy.wait()
    outer(s0, s1, 0)
    pack_y(s1)
    pack_z(s1)
    halo1 = halos(s1, 1)
    inner(s1, out)
    for copy in mid_copies:
        copy.wait_recv()
    expand(1)
    for copy in halo1:
        copy.wait()
    outer(s1, out, 1)

    for f in range(5):
        for a in range(8):
            total = None
            for x in range(2):
                for y in range(2):
                    piece = out[f, pl.ds((2 * a + x) * BS + y, 8, stride=2), :]
                    total = piece if total is None else total + piece
            xy[pl.ds((f * 8 + a) * 8, 8), :] = 0.125 * total
    used = 5 * 64
    interleave = (iota((LANES, 8 * LANES), 0) == iota((LANES, 8 * LANES), 1) // 8).astype(F32).astype(BF16)
    lane8 = iota((blk, LANES), 1) % 8
    sel = beside(sel_tk, blk)
    back = []
    for c in range((used + LANES - 1) // LANES):
        size = min(LANES, used - c * LANES)
        block = xy[pl.ds(c * LANES, LANES), :]
        if size < LANES:
            block = jnp.where(iota((LANES, LANES), 0) < size, block, 0.0)
        zt[...] = block.T
        rows = jnp.concatenate(
            [zt[pl.ds(2 * z, blk, stride=BS), :] + zt[pl.ds(2 * z + 1, blk, stride=BS), :] for z in range(8)],
            axis=0,
        )
        wide = dot(jnp.concatenate(parts_of(rows, 3), axis=0).astype(BF16), interleave, ((1,), (0,)))
        wide = wide[:64] + wide[64:128] + wide[128:]
        tiles = []
        for g in range(size // 16):
            tile = wide[0:8, g * LANES:(g + 1) * LANES]
            for z in range(1, 8):
                tile = jnp.where(lane8 == z, wide[z * 8:z * 8 + 8, g * LANES:(g + 1) * LANES], tile)
            tiles.append(tile)
        routed = dot(sel, stacked(jnp.concatenate(tiles, axis=1)), ((1,), (0,)))
        stage, first, each = (rstage, 0, 8) if c == 0 else (rstage2, (c - 1) * 8, rchunks - 8)
        for g in range(size // 16):
            stage[pl.ds(first + g, count, stride=each), :] = routed[:, g * LANES:(g + 1) * LANES]
        if c == 0:
            back.append(exchange(2, rstage, rrecv, 2 * 8))
    back.append(exchange(3, rstage2, rrecv2, 2 * (rchunks - 8)))
    sel = beside(sel_st, count)
    for half, (recv, first, each) in enumerate(((rrecv, 0, 8), (rrecv2, 8, rchunks - 8))):
        for copy in back[half]:
            copy.wait_recv()
        for c in range(each):
            rows = recv[pl.ds(c, count, stride=each), :]
            coarse[0, :, pl.ds((first + c) * LANES, LANES)] = dot(sel, stacked(rows), ((1,), (0,)))
    for copy in now_copies + mid_copies + back[0] + back[1]:
        copy.wait_send()


def place(out, coarse, out_new, coarse_new, sem):
    copies = [pltpu.make_async_copy(out.at[f], out_new.at[f], sem.at[f]) for f in range(5)]
    copies.append(pltpu.make_async_copy(coarse, coarse_new, sem.at[5]))
    for copy in copies:
        copy.start()
    for copy in copies:
        copy.wait()


def shards(n, fine, shell, parent, link):
    group = n[1] * n[2]
    count = 2 * group
    rwidth = 5 * (BS // 2) ** 3
    fine2 = fine.reshape(5, BS * BS, LANES)
    vmem = pl.BlockSpec(memory_space=pltpu.VMEM)
    out, coarse = pl.pallas_call(
        functools.partial(kernel, n),
        out_shape=(
            pltpu.VMEM((5, BS * BS, LANES), F32),
            pltpu.VMEM((1, shell.shape[1], rwidth), F32),
        ),
        in_specs=[pl.BlockSpec(memory_space=pltpu.HBM)] * 4,
        out_specs=(vmem, vmem),
        scratch_shapes=[
            pltpu.VMEM(shell.shape, F32),
            pltpu.VMEM(parent.shape, jnp.int32),
            pltpu.VMEM(link.shape, jnp.int32),
            pltpu.VMEM((5, BS * BS, LANES), F32),
            pltpu.VMEM((5, BS * BS, LANES), F32),
            pltpu.VMEM((2, 5, BS, LANES), F32),
            pltpu.VMEM((2, BS, LANES), F32),
            pltpu.VMEM((2, 2, 5, BS, LANES), F32),
            pltpu.VMEM((2, 2, 5, BS, LANES), F32),
            pltpu.VMEM((2, 2, 2, BS, LANES), F32),
            pltpu.VMEM((2, count * 16, LANES), F32),
            pltpu.VMEM((2, count * 16, LANES), F32),
            pltpu.VMEM((count * 8, LANES), F32),
            pltpu.VMEM((count * 8, LANES), F32),
            pltpu.VMEM((count * (rwidth // LANES - 8), LANES), F32),
            pltpu.VMEM((count * (rwidth // LANES - 8), LANES), F32),
            pltpu.VMEM((1920, LANES), F32),
            pltpu.VMEM((20 * BS, LANES), F32),
            pltpu.VMEM((10 * BS, LANES), F32),
            pltpu.VMEM((10, BS, LANES), F32),
            pltpu.VMEM((384, LANES), F32),
            pltpu.VMEM((LANES, LANES), F32),
            pltpu.SemaphoreType.DMA((8,)),
            pltpu.SemaphoreType.DMA((2, 6)),
            pltpu.SemaphoreType.DMA((2, 6)),
            pltpu.SemaphoreType.DMA((4, group)),
            pltpu.SemaphoreType.DMA((4, group)),
        ],
        compiler_params=pltpu.CompilerParams(
            collective_id=0, has_side_effects=True, vmem_limit_bytes=62 * 1024 * 1024
        ),
    )(fine2, shell, parent, link)
    hbm = pl.BlockSpec(memory_space=pltpu.HBM)
    out, coarse = pl.pallas_call(
        place,
        out_shape=(jax.ShapeDtypeStruct(out.shape, F32), jax.ShapeDtypeStruct(coarse.shape, F32)),
        in_specs=[vmem, vmem],
        out_specs=(hbm, hbm),
        scratch_shapes=[pltpu.SemaphoreType.DMA((6,))],
        compiler_params=pltpu.CompilerParams(vmem_limit_bytes=4 * 1024 * 1024),
    )(out, coarse)
    return out.reshape(fine.shape), coarse


def solution(mesh):
    n = (mesh.shape["gx"], mesh.shape["gy"], mesh.shape["gz"])
    return jax.shard_map(
        functools.partial(shards, n),
        mesh=mesh,
        in_specs=(
            P(None, "gx", "gy", "gz"),
            P("gx", ("gy", "gz"), None),
            P("gx", None),
            P(None, "gx", "gy", "gz"),
        ),
        out_specs=(P(None, "gx", "gy", "gz"), P("gx", ("gy", "gz"), None)),
        check_vma=False,
    )
```

```python
import functools

import jax
import jax.numpy as jnp
from jax import lax
from jax.experimental import pallas as pl
from jax.experimental.pallas import tpu as pltpu
from jax.sharding import PartitionSpec as P

BS = 16
GAMMA = 1.4
LAMBDA = 0.05
LANES = 128
MESH = pl.DeviceIdType.MESH
F32 = jnp.float32
BF16 = jnp.bfloat16


def iota(shape, dim):
    return lax.broadcasted_iota(jnp.int32, shape, dim)


def parts_of(x, count):
    result = []
    for _ in range(count - 1):
        head = x.astype(BF16).astype(F32)
        result.append(head)
        x = x - head
    result.append(x)
    return result


def dot(a, b, contract):
    return lax.dot_general(a, b, (contract, ((), ())), preferred_element_type=F32)


def stacked(x):
    pieces = parts_of(x, 3)
    if x.shape[0] % 16:
        pieces.append(jnp.zeros_like(x))
    return jnp.concatenate(pieces, axis=0).astype(BF16)


def beside(x, rows):
    count = 4 if rows % 16 else 3
    return jnp.concatenate([x] * count, axis=1).astype(BF16)


def prim(u):
    inv = 1.0 / u[0]
    vel = [u[1] * inv, u[2] * inv, u[3] * inv]
    press = (GAMMA - 1.0) * (u[4] - 0.5 * (u[1] * vel[0] + u[2] * vel[1] + u[3] * vel[2]))
    sound = jnp.sqrt(GAMMA * press * inv)
    return vel, press, sound


def flux(u, pr, d):
    vel, press, sound = pr
    vd = vel[d]
    f = [u[1 + d], u[1] * vd, u[2] * vd, u[3] * vd, (u[4] + press) * vd]
    f[1 + d] = f[1 + d] + press
    return f, jnp.abs(vd) + sound


def interface(ul, fl, sl, ur, fr, sr, sign=None):
    wave = jnp.maximum(sl, sr)
    if sign is not None:
        wave = sign * wave
    return [(fl[i] + fr[i]) - wave * (ur[i] - ul[i]) for i in range(5)]


def kernel(
    n,
    fine, shell_hbm, parent_hbm, link_hbm, out, coarse,
    shell, parent, link, s0, s1, ypack, zpack, hx, hy, hz, sstage, srecv, rstage, rrecv, rstage2, rrecv2, xt, cxy, cz, cells_z, xy, zt,
    load_sem, halo_send, halo_recv, all_send, all_recv,
):
    nx, ny, nz = n
    group = ny * nz
    count = 2 * group
    gx, gy, gz = lax.axis_index("gx"), lax.axis_index("gy"), lax.axis_index("gz")
    me = gy * nz + gz
    blk = shell.shape[1]
    width = shell.shape[2] // 2
    chunks = width // LANES
    rwidth = coarse.shape[2]
    rchunks = rwidth // LANES
    nq = parent.shape[1]
    peers = []
    order = sorted(range(1, group), key=lambda i: i % nz == 0)
    for i in order:
        peer = lax.rem(me + i, group)
        peers.append((gx, peer // nz, lax.rem(peer, nz)))
    xlo, xhi = (lax.rem(gx + nx - 1, nx), gy, gz), (lax.rem(gx + 1, nx), gy, gz)
    ylo, yhi = (gx, lax.rem(gy + ny - 1, ny), gz), (gx, lax.rem(gy + 1, ny), gz)
    zlo, zhi = (gx, gy, lax.rem(gz + nz - 1, nz)), (gx, gy, lax.rem(gz + 1, nz))

    barrier = pltpu.get_barrier_semaphore()
    greeted = peers + [xlo, xhi]
    for dev in greeted:
        pl.semaphore_signal(barrier, inc=1, device_id=dev, device_id_type=MESH)

    loads = []
    for k, (src, dst) in enumerate(((parent_hbm, parent), (shell_hbm, shell), (link_hbm, link))):
        load = pltpu.make_async_copy(src, dst, load_sem.at[5 + k])
        load.start()
        loads.append(load)
    for f in range(5):
        load = pltpu.make_async_copy(fine.at[f], s0.at[f], load_sem.at[f])
        load.start()
        loads.append(load)

    loads[0].wait()
    par = parent[...]
    lane_q = iota((1, nq), 1)
    owner = par // blk
    rank = jnp.zeros((1, nq), jnp.int32)
    for j in range(1, blk):
        before = pltpu.roll(jnp.broadcast_to(owner, (8, nq)), j, 1)[0:1]
        rank = rank + jnp.where((lane_q % blk >= j) & (before == owner), 1, 0)
    at_owner = (lane_q // blk) * 2 + rank
    at_block = owner * 2 + rank
    to_t = (jnp.broadcast_to(at_owner, (count, nq)) == iota((count, nq), 0)).astype(F32).astype(BF16)
    mine = (jnp.broadcast_to(par, (blk, nq)) == me * blk + iota((blk, nq), 0)).astype(F32).astype(BF16)
    sel_ts = dot(to_t, mine, ((1,), (1,)))

    loads[1].wait()
    sel = beside(sel_ts, blk)

    def stage_level(level):
        for c in range(chunks):
            value = shell[0, :, pl.ds(c * LANES, LANES)]
            if level:
                value = 0.5 * (value + shell[0, :, pl.ds(width + c * LANES, LANES)])
            sstage[level, pl.ds(c, count, stride=16), :] = dot(sel, stacked(value), ((1,), (0,)))

    stage_level(0)

    lane = iota((BS, LANES), 1)
    sub = iota((BS, LANES), 0)
    even = lane % 2 == 0
    pair = ((lane + 1) // 2) % 8
    first_pairs = (lane + 1) % LANES < 16

    def plane(ref, f, x):
        return ref[f, pl.ds(x * BS, BS), :]

    def pack_y(ref, step):
        for f in range(5):
            ypack[step, 0, f] = ref[f, pl.ds(0, BS, stride=BS), :]
            ypack[step, 1, f] = ref[f, pl.ds(BS - 1, BS, stride=BS), :]

    def pack_z(ref, step):
        packed = [jnp.zeros((BS, LANES), F32)] * 2
        for f in range(5):
            for g in range(2):
                tile = plane(ref, f, 8 * g)
                for x in range(1, 8):
                    tile = jnp.where(pair == x, pltpu.roll(plane(ref, f, 8 * g + x), 2 * x, 1), tile)
                k = f * 2 + g
                cells_z[k] = tile
                moved = tile if k % 8 == 0 else pltpu.roll(tile, 16 * (k % 8), 1)
                packed[k // 8] = jnp.where(((lane + 1) // 16) % 8 == k % 8, moved, packed[k // 8])
        zpack[step, 0] = packed[0]
        zpack[step, 1] = packed[1]

    def halos(ref, step):
        copies = []

        def send(k, src, dst, dev):
            copy = pltpu.make_async_remote_copy(
                src_ref=src, dst_ref=dst, send_sem=halo_send.at[step, k], recv_sem=halo_recv.at[step, k],
                device_id=dev, device_id_type=MESH,
            )
            copy.start()
            copies.append(copy)

        send(0, ref.at[:, pl.ds(BS * BS - BS, BS)], hx.at[step, 0], xhi)
        send(1, ref.at[:, pl.ds(0, BS)], hx.at[step, 1], xlo)
        pack_z(ref, step)
        send(4, zpack.at[step], hz.at[step, 0], zhi)
        send(5, zpack.at[step], hz.at[step, 1], zlo)
        pack_y(ref, step)
        send(2, ypack.at[step, 1], hy.at[step, 0], yhi)
        send(3, ypack.at[step, 0], hy.at[step, 1], ylo)
        return copies

    def exchange(kind, stage, recv, rows):
        copies = []
        for i, dev in zip(order, peers):
            to = lax.rem(me + i, group)
            copy = pltpu.make_async_remote_copy(
                src_ref=stage.at[pl.ds(pl.multiple_of(to * rows, 8), rows)],
                dst_ref=recv.at[pl.ds(pl.multiple_of(me * rows, 8), rows)],
                send_sem=all_send.at[kind, i], recv_sem=all_recv.at[kind, i],
                device_id=dev, device_id_type=MESH,
            )
            copy.start()
            copies.append(copy)
        own = pl.ds(pl.multiple_of(me * rows, 8), rows)
        recv[own, :] = stage[own, :]
        return copies

    for load in loads[2:]:
        load.wait()
    pl.semaphore_wait(barrier, len(greeted))
    now_copies = exchange(0, sstage.at[0], srecv.at[0], 32)
    halo0 = halos(s0, 0)

    sel_st = dot(mine, to_t, ((1,), (1,)))
    at_block8 = jnp.broadcast_to(at_block.astype(F32), (8, nq)).astype(BF16)
    spread = (iota((nq, LANES), 0) == me * blk + iota((nq, LANES), 1) // BS).astype(F32).astype(BF16)
    pick = (iota((nq, blk), 0) == me * blk + iota((nq, blk), 1)).astype(F32).astype(BF16)
    row_lane = dot(at_block8, spread, ((1,), (0,)))[0:1]
    block_hi = ((iota((nq, LANES), 1) + 1) // BS + blk - 1) % blk
    spread_hi = (iota((nq, LANES), 0) == me * blk + block_hi).astype(F32).astype(BF16)
    row_lane_hi = dot(at_block8, spread_hi, ((1,), (0,)))[0:1]
    row_blk = dot(at_block8, pick, ((1,), (0,)))[0:1]
    be = (jnp.broadcast_to(row_lane, (count, LANES)) == iota((count, LANES), 0).astype(F32)).astype(F32)
    be3 = jnp.concatenate([be] * 3, axis=0).astype(BF16)
    be_hi = (jnp.broadcast_to(row_lane_hi, (count, LANES)) == iota((count, LANES), 0).astype(F32)).astype(F32)
    be3_hi = jnp.concatenate([be_hi] * 3, axis=0).astype(BF16)
    sel_tk = (jnp.broadcast_to(row_blk, (count, blk)) == iota((count, blk), 0).astype(F32)).astype(F32)


    linkf = jnp.concatenate([link[k, 0] for k in range(6)] + [jnp.zeros((2, blk), jnp.int32)], axis=0)
    over = (iota((blk, LANES), 0) == iota((blk, LANES), 1) // BS).astype(F32).astype(BF16)
    over_hi = (iota((blk, LANES), 0) == ((iota((blk, LANES), 1) + 1) // BS + blk - 1) % blk).astype(F32).astype(BF16)
    linkb = linkf.astype(F32).astype(BF16)
    mask = dot(linkb, over, ((1,), (0,)))
    mask_hi = dot(linkb, over_hi, ((1,), (0,)))
    is_lo = lane % BS == 0
    at_end = is_lo | (lane % BS == BS - 1)
    zmask = jnp.where(even, mask[4:5], mask_hi[5:6]) > 0.5
    half_lane = (iota((8, LANES), 1) % BS) // 2
    even8 = iota((8, LANES), 1) % 2 == 0
    pair8 = (((iota((8, LANES), 1) + 1) // 2) % 8) // 2

    def expand(level):
        for c in range(chunks):
            rows = stacked(srecv[level, pl.ds(c, count, stride=16), :])
            if c * LANES < 1600:
                xt[pl.ds(c * LANES, LANES), :] = dot(rows, be3, ((0,), (0,)))
            if (c + 1) * LANES > 1600:
                skip = max(0, 1600 - c * LANES)
                xt[pl.ds(c * LANES + skip, LANES - skip), :] = dot(rows, be3_hi, ((0,), (0,)))[skip:]
        for k in range(20):
            tile = xt[pl.ds(k * 64, 8, stride=8), :]
            for b in range(1, 8):
                tile = jnp.where(half_lane == b, xt[pl.ds(k * 64 + b, 8, stride=8), :], tile)
            cxy[pl.ds(k * BS, 8, stride=2), :] = tile
            cxy[pl.ds(k * BS + 1, 8, stride=2), :] = tile
        for k in range(10):
            tile = None
            for a in range(4):
                at = ((k // 2) * 8 + 4 * (k % 2) + a) * 8
                piece = jnp.where(even8, xt[pl.ds(1280 + at, 8), :], xt[pl.ds(1600 + at, 8), :])
                tile = piece if a == 0 else jnp.where(pair8 == a, piece, tile)
            cz[pl.ds(k * BS, 8, stride=2), :] = tile
            cz[pl.ds(k * BS + 1, 8, stride=2), :] = tile

    def inner(ref, dst):
        def step_x(x, hxl, u, pr, last):
            if last:
                total = [-hxl[f] for f in range(5)]
                hxr, un, prn = hxl, u, pr
            else:
                at = pl.multiple_of((x + 1) * BS, BS)
                un = [ref[f, pl.ds(at, BS), :] for f in range(5)]
                prn = prim(un)
                fc, sc = flux(u, pr, 0)
                fn, sn = flux(un, prn, 0)
                hxr = interface(u, fc, sc, un, fn, sn)
                total = [hxr[f] - hxl[f] for f in range(5)]
            for d, axis, edge in ((1, 0, sub == 0), (2, 1, is_lo)):
                fc, sc = flux(u, pr, d)
                ub = [pltpu.roll(a, 1, axis) for a in u]
                fb = [pltpu.roll(a, 1, axis) for a in fc]
                low = interface(ub, fb, pltpu.roll(sc, 1, axis), u, fc, sc)
                for f in range(5):
                    lo = jnp.where(edge, 0.0, low[f])
                    total[f] = total[f] + (pltpu.roll(lo, lo.shape[axis] - 1, axis) - lo)
            at = pl.multiple_of(x * BS, BS)
            for f in range(5):
                dst[f, pl.ds(at, BS), :] = u[f] - (0.5 * LAMBDA) * total[f]
            return hxr, un, prn

        u = [plane(ref, f, 0) for f in range(5)]
        zero = [jnp.zeros((BS, LANES), F32)] * 5
        carry = lax.fori_loop(
            0, BS - 1, lambda x, carry: step_x(x, *carry, False), (zero, u, prim(u)), unroll=3
        )
        step_x(BS - 1, *carry, True)

    def faces(ghost, cells, d, sign):
        gf, gs = flux(ghost, prim(ghost), d)
        cf, cs = flux(cells, prim(cells), d)
        return interface(ghost, gf, gs, cells, cf, cs, sign)

    def outer(ref, dst, step, after):
        for d in range(2):
            for side in range(2):
                chosen = jnp.broadcast_to(mask[2 * d + side:2 * d + side + 1], (BS, LANES)) > 0.5
                halo = hx if d == 0 else hy
                if d == 0:
                    rows = pl.ds(side * (BS - 1) * BS, BS)
                else:
                    rows = pl.ds(side * (BS - 1), BS, stride=BS)
                ghost = [
                    jnp.where(chosen, halo[step, side, f], cxy[pl.ds(((2 * d + side) * 5 + f) * BS, BS), :])
                    for f in range(5)
                ]
                cells = [ref[f, rows, :] for f in range(5)]
                face = faces(ghost, cells, d, 1.0 - 2 * side)
                for f in range(5):
                    dst[f, rows, :] = dst[f, rows, :] + (0.5 - side) * LAMBDA * face[f]
        comb = []
        for k in range(2):
            left = pltpu.roll(hz[step, 0, k], 1, 1)
            right = pltpu.roll(hz[step, 1, k], LANES - 1, 1)
            comb.append(jnp.where(even, left, right))
        sign = jnp.where(even, 1.0, -1.0)
        scale = (0.5 * LAMBDA) * sign
        for g in range(2):
            cells, ghost = [], []
            for f in range(5):
                k = f * 2 + g
                tile = cells_z[k]
                near = jnp.where(even, pltpu.roll(tile, 1, 1), pltpu.roll(tile, LANES - 1, 1))
                far = comb[k // 8]
                if k % 8:
                    far = pltpu.roll(far, LANES - 16 * (k % 8), 1)
                fine_side = jnp.where(first_pairs, far, near)
                cells.append(tile)
                ghost.append(jnp.where(zmask, fine_side, cz[pl.ds(k * BS, BS), :]))
            face = faces(ghost, cells, 2, sign)
            for f in range(5):
                change = scale * face[f]
                for x in range(8):
                    moved = change if x == 0 else pltpu.roll(change, LANES - 2 * x, 1)
                    rows = pl.ds((8 * g + x) * BS, BS)
                    dst[f, rows, :] = dst[f, rows, :] + jnp.where(at_end, moved, 0.0)
            after(g)

    inner(s0, s1)
    stage_level(1)
    mid_copies = exchange(1, sstage.at[1], srecv.at[1], 32)
    for copy in now_copies:
        copy.wait_recv()
    expand(0)
    for copy in halo0:
        copy.wait()
    outer(s0, s1, 0, lambda g: None)
    halo1 = halos(s1, 1)
    inner(s1, out)
    for copy in mid_copies:
        copy.wait_recv()
    expand(1)
    for copy in halo1:
        copy.wait()
    interleave = (iota((LANES, 8 * LANES), 0) == iota((LANES, 8 * LANES), 1) // 8).astype(F32).astype(BF16)
    lane8 = iota((blk, LANES), 1) % 8
    used = 5 * 64
    sel_rows = beside(sel_tk, blk)

    def means(g):
        for f in range(5):
            for a in range(4):
                total = None
                for x in range(2):
                    for y in range(2):
                        piece = out[f, pl.ds((8 * g + 2 * a + x) * BS + y, 8, stride=2), :]
                        total = piece if total is None else total + piece
                xy[pl.ds(g * 160 + f * 32 + a * 8, 8), :] = 0.125 * total

    def rows_out(c):
        size = min(LANES, used - c * LANES)
        block = xy[pl.ds(c * LANES, LANES), :]
        if size < LANES:
            block = jnp.where(iota((LANES, LANES), 0) < size, block, 0.0)
        zt[...] = block.T
        rows = jnp.concatenate(
            [zt[pl.ds(2 * z, blk, stride=BS), :] + zt[pl.ds(2 * z + 1, blk, stride=BS), :] for z in range(8)],
            axis=0,
        )
        wide = dot(jnp.concatenate(parts_of(rows, 3), axis=0).astype(BF16), interleave, ((1,), (0,)))
        wide = wide[:64] + wide[64:128] + wide[128:]
        tiles = []
        for g in range(size // 16):
            tile = wide[0:8, g * LANES:(g + 1) * LANES]
            for z in range(1, 8):
                tile = jnp.where(lane8 == z, wide[z * 8:z * 8 + 8, g * LANES:(g + 1) * LANES], tile)
            tiles.append(tile)
        routed = dot(sel_rows, stacked(jnp.concatenate(tiles, axis=1)), ((1,), (0,)))
        stage, first, each = (rstage, 0, 8) if c == 0 else (rstage2, (c - 1) * 8, rchunks - 8)
        for g in range(size // 16):
            stage[pl.ds(first + g, count, stride=each), :] = routed[:, g * LANES:(g + 1) * LANES]

    back = []

    def after(g):
        means(g)
        if g == 0:
            rows_out(0)
            back.append(exchange(2, rstage, rrecv, 2 * 8))
        else:
            rows_out(1)
            rows_out(2)
            back.append(exchange(3, rstage2, rrecv2, 2 * (rchunks - 8)))

    outer(s1, out, 1, after)
    sel = beside(sel_st, count)
    for half, (recv, first, each) in enumerate(((rrecv, 0, 8), (rrecv2, 8, rchunks - 8))):
        for copy in back[half]:
            copy.wait_recv()
        for c in range(each):
            rows = recv[pl.ds(c, count, stride=each), :]
            start = (first + c) * 16
            g, f, pairs = start // 160, start % 160 // 32, start % 32 // 16
            coarse[0, :, pl.ds((f * 4 + 2 * g + pairs) * LANES, LANES)] = dot(sel, stacked(rows), ((1,), (0,)))
    for copy in now_copies + mid_copies + back[0] + back[1]:
        copy.wait_send()


def place(out, coarse, out_new, coarse_new, sem):
    copies = [pltpu.make_async_copy(out.at[f], out_new.at[f], sem.at[f]) for f in range(5)]
    copies.append(pltpu.make_async_copy(coarse, coarse_new, sem.at[5]))
    for copy in copies:
        copy.start()
    for copy in copies:
        copy.wait()


def shards(n, fine, shell, parent, link):
    group = n[1] * n[2]
    count = 2 * group
    rwidth = 5 * (BS // 2) ** 3
    fine2 = fine.reshape(5, BS * BS, LANES)
    vmem = pl.BlockSpec(memory_space=pltpu.VMEM)
    out, coarse = pl.pallas_call(
        functools.partial(kernel, n),
        out_shape=(
            pltpu.VMEM((5, BS * BS, LANES), F32),
            pltpu.VMEM((1, shell.shape[1], rwidth), F32),
        ),
        in_specs=[pl.BlockSpec(memory_space=pltpu.HBM)] * 4,
        out_specs=(vmem, vmem),
        scratch_shapes=[
            pltpu.VMEM(shell.shape, F32),
            pltpu.VMEM(parent.shape, jnp.int32),
            pltpu.VMEM(link.shape, jnp.int32),
            pltpu.VMEM((5, BS * BS, LANES), F32),
            pltpu.VMEM((5, BS * BS, LANES), F32),
            pltpu.VMEM((2, 2, 5, BS, LANES), F32),
            pltpu.VMEM((2, 2, BS, LANES), F32),
            pltpu.VMEM((2, 2, 5, BS, LANES), F32),
            pltpu.VMEM((2, 2, 5, BS, LANES), F32),
            pltpu.VMEM((2, 2, 2, BS, LANES), F32),
            pltpu.VMEM((2, count * 16, LANES), F32),
            pltpu.VMEM((2, count * 16, LANES), F32),
            pltpu.VMEM((count * 8, LANES), F32),
            pltpu.VMEM((count * 8, LANES), F32),
            pltpu.VMEM((count * (rwidth // LANES - 8), LANES), F32),
            pltpu.VMEM((count * (rwidth // LANES - 8), LANES), F32),
            pltpu.VMEM((1920, LANES), F32),
            pltpu.VMEM((20 * BS, LANES), F32),
            pltpu.VMEM((10 * BS, LANES), F32),
            pltpu.VMEM((10, BS, LANES), F32),
            pltpu.VMEM((384, LANES), F32),
            pltpu.VMEM((LANES, LANES), F32),
            pltpu.SemaphoreType.DMA((8,)),
            pltpu.SemaphoreType.DMA((2, 6)),
            pltpu.SemaphoreType.DMA((2, 6)),
            pltpu.SemaphoreType.DMA((4, group)),
            pltpu.SemaphoreType.DMA((4, group)),
        ],
        compiler_params=pltpu.CompilerParams(
            collective_id=0, has_side_effects=True, vmem_limit_bytes=62 * 1024 * 1024
        ),
    )(fine2, shell, parent, link)
    hbm = pl.BlockSpec(memory_space=pltpu.HBM)
    out, coarse = pl.pallas_call(
        place,
        out_shape=(jax.ShapeDtypeStruct(out.shape, F32), jax.ShapeDtypeStruct(coarse.shape, F32)),
        in_specs=[vmem, vmem],
        out_specs=(hbm, hbm),
        scratch_shapes=[pltpu.SemaphoreType.DMA((6,))],
        compiler_params=pltpu.CompilerParams(vmem_limit_bytes=4 * 1024 * 1024),
    )(out, coarse)
    return out.reshape(fine.shape), coarse


def solution(mesh):
    n = (mesh.shape["gx"], mesh.shape["gy"], mesh.shape["gz"])
    return jax.shard_map(
        functools.partial(shards, n),
        mesh=mesh,
        in_specs=(
            P(None, "gx", "gy", "gz"),
            P("gx", ("gy", "gz"), None),
            P("gx", None),
            P(None, "gx", "gy", "gz"),
        ),
        out_specs=(P(None, "gx", "gy", "gz"), P("gx", ("gy", "gz"), None)),
        check_vma=False,
    )
```

```python
import functools

import jax
import jax.numpy as jnp
from jax import lax
from jax.experimental import pallas as pl
from jax.experimental.pallas import tpu as pltpu
from jax.sharding import PartitionSpec as P

BS = 16
GAMMA = 1.4
LAMBDA = 0.05
LANES = 128
MESH = pl.DeviceIdType.MESH
F32 = jnp.float32
BF16 = jnp.bfloat16


def iota(shape, dim):
    return lax.broadcasted_iota(jnp.int32, shape, dim)


def parts_of(x, count):
    result = []
    for _ in range(count - 1):
        head = x.astype(BF16).astype(F32)
        result.append(head)
        x = x - head
    result.append(x)
    return result


def dot(a, b, contract):
    return lax.dot_general(a, b, (contract, ((), ())), preferred_element_type=F32)


def stacked(x):
    pieces = parts_of(x, 3)
    if x.shape[0] % 16:
        pieces.append(jnp.zeros_like(x))
    return jnp.concatenate(pieces, axis=0).astype(BF16)


def beside(x, rows):
    count = 4 if rows % 16 else 3
    return jnp.concatenate([x] * count, axis=1).astype(BF16)


def prim(u):
    inv = 1.0 / u[0]
    vel = [u[1] * inv, u[2] * inv, u[3] * inv]
    press = (GAMMA - 1.0) * (u[4] - 0.5 * (u[1] * vel[0] + u[2] * vel[1] + u[3] * vel[2]))
    sound = jnp.sqrt(GAMMA * press * inv)
    return vel, press, sound


def flux(u, pr, d):
    vel, press, sound = pr
    vd = vel[d]
    f = [u[1 + d], u[1] * vd, u[2] * vd, u[3] * vd, (u[4] + press) * vd]
    f[1 + d] = f[1 + d] + press
    return f, jnp.abs(vd) + sound


def interface(ul, fl, sl, ur, fr, sr, sign=None):
    wave = jnp.maximum(sl, sr)
    if sign is not None:
        wave = sign * wave
    return [(fl[i] + fr[i]) - wave * (ur[i] - ul[i]) for i in range(5)]


def kernel(
    n,
    fine, shell_hbm, parent_hbm, link_hbm, out, coarse,
    shell, parent, link, s0, s1, ypack, zpack, hx, hy, hz, sstage, srecv, rstage, rrecv, rstage2, rrecv2, xt, cxy, cz, cells_z, xy, zt,
    load_sem, halo_send, halo_recv, all_send, all_recv,
):
    nx, ny, nz = n
    group = ny * nz
    count = 2 * group
    gx, gy, gz = lax.axis_index("gx"), lax.axis_index("gy"), lax.axis_index("gz")
    me = gy * nz + gz
    blk = shell.shape[1]
    width = shell.shape[2] // 2
    chunks = width // LANES
    rwidth = coarse.shape[2]
    rchunks = rwidth // LANES
    nq = parent.shape[1]
    peers = []
    order = sorted(range(1, group), key=lambda i: i % nz == 0)
    for i in order:
        peer = lax.rem(me + i, group)
        peers.append((gx, peer // nz, lax.rem(peer, nz)))
    xlo, xhi = (lax.rem(gx + nx - 1, nx), gy, gz), (lax.rem(gx + 1, nx), gy, gz)
    ylo, yhi = (gx, lax.rem(gy + ny - 1, ny), gz), (gx, lax.rem(gy + 1, ny), gz)
    zlo, zhi = (gx, gy, lax.rem(gz + nz - 1, nz)), (gx, gy, lax.rem(gz + 1, nz))

    barrier = pltpu.get_barrier_semaphore()
    greeted = peers + [xlo, xhi]
    for dev in greeted:
        pl.semaphore_signal(barrier, inc=1, device_id=dev, device_id_type=MESH)

    loads = []
    for k, (src, dst) in enumerate(((parent_hbm, parent), (shell_hbm, shell), (link_hbm, link))):
        load = pltpu.make_async_copy(src, dst, load_sem.at[5 + k])
        load.start()
        loads.append(load)
    for f in range(5):
        load = pltpu.make_async_copy(fine.at[f], s0.at[f], load_sem.at[f])
        load.start()
        loads.append(load)

    loads[0].wait()
    par = parent[...]
    lane_q = iota((1, nq), 1)
    owner = par // blk
    rank = jnp.zeros((1, nq), jnp.int32)
    for j in range(1, blk):
        before = pltpu.roll(jnp.broadcast_to(owner, (8, nq)), j, 1)[0:1]
        rank = rank + jnp.where((lane_q % blk >= j) & (before == owner), 1, 0)
    at_owner = (lane_q // blk) * 2 + rank
    at_block = owner * 2 + rank
    to_t = (jnp.broadcast_to(at_owner, (count, nq)) == iota((count, nq), 0)).astype(F32).astype(BF16)
    mine = (jnp.broadcast_to(par, (blk, nq)) == me * blk + iota((blk, nq), 0)).astype(F32).astype(BF16)
    sel_ts = dot(to_t, mine, ((1,), (1,)))

    loads[1].wait()
    sel = beside(sel_ts, blk)

    def stage_level(level):
        for c in range(chunks):
            value = shell[0, :, pl.ds(c * LANES, LANES)]
            if level:
                value = 0.5 * (value + shell[0, :, pl.ds(width + c * LANES, LANES)])
            sstage[level, pl.ds(c, count, stride=16), :] = dot(sel, stacked(value), ((1,), (0,)))

    stage_level(0)

    lane = iota((BS, LANES), 1)
    sub = iota((BS, LANES), 0)
    even = lane % 2 == 0
    pair = ((lane + 1) // 2) % 8
    first_pairs = (lane + 1) % LANES < 16

    def plane(ref, f, x):
        return ref[f, pl.ds(x * BS, BS), :]

    def pack_y(ref, step):
        for f in range(5):
            ypack[step, 0, f] = ref[f, pl.ds(0, BS, stride=BS), :]
            ypack[step, 1, f] = ref[f, pl.ds(BS - 1, BS, stride=BS), :]

    def pack_z(ref, step):
        packed = [jnp.zeros((BS, LANES), F32)] * 2
        for f in range(5):
            for g in range(2):
                tile = plane(ref, f, 8 * g)
                for x in range(1, 8):
                    tile = jnp.where(pair == x, pltpu.roll(plane(ref, f, 8 * g + x), 2 * x, 1), tile)
                k = f * 2 + g
                cells_z[k] = tile
                moved = tile if k % 8 == 0 else pltpu.roll(tile, 16 * (k % 8), 1)
                packed[k // 8] = jnp.where(((lane + 1) // 16) % 8 == k % 8, moved, packed[k // 8])
        zpack[step, 0] = packed[0]
        zpack[step, 1] = packed[1]

    def halos(ref, step):
        copies = []

        def send(k, src, dst, dev):
            copy = pltpu.make_async_remote_copy(
                src_ref=src, dst_ref=dst, send_sem=halo_send.at[step, k], recv_sem=halo_recv.at[step, k],
                device_id=dev, device_id_type=MESH,
            )
            copy.start()
            copies.append(copy)

        send(0, ref.at[:, pl.ds(BS * BS - BS, BS)], hx.at[step, 0], xhi)
        send(1, ref.at[:, pl.ds(0, BS)], hx.at[step, 1], xlo)
        pack_z(ref, step)
        send(4, zpack.at[step], hz.at[step, 0], zhi)
        send(5, zpack.at[step], hz.at[step, 1], zlo)
        pack_y(ref, step)
        send(2, ypack.at[step, 1], hy.at[step, 0], yhi)
        send(3, ypack.at[step, 0], hy.at[step, 1], ylo)
        return copies

    def exchange(kind, stage, recv, rows):
        copies = []
        for i, dev in zip(order, peers):
            to = lax.rem(me + i, group)
            copy = pltpu.make_async_remote_copy(
                src_ref=stage.at[pl.ds(pl.multiple_of(to * rows, 8), rows)],
                dst_ref=recv.at[pl.ds(pl.multiple_of(me * rows, 8), rows)],
                send_sem=all_send.at[kind, i], recv_sem=all_recv.at[kind, i],
                device_id=dev, device_id_type=MESH,
            )
            copy.start()
            copies.append(copy)
        own = pl.ds(pl.multiple_of(me * rows, 8), rows)
        recv[own, :] = stage[own, :]
        return copies

    for load in loads[2:]:
        load.wait()
    pl.semaphore_wait(barrier, len(greeted))
    now_copies = exchange(0, sstage.at[0], srecv.at[0], 32)
    halo0 = halos(s0, 0)

    sel_st = dot(mine, to_t, ((1,), (1,)))
    at_block8 = jnp.broadcast_to(at_block.astype(F32), (8, nq)).astype(BF16)
    spread = (iota((nq, LANES), 0) == me * blk + iota((nq, LANES), 1) // BS).astype(F32).astype(BF16)
    pick = (iota((nq, blk), 0) == me * blk + iota((nq, blk), 1)).astype(F32).astype(BF16)
    row_lane = dot(at_block8, spread, ((1,), (0,)))[0:1]
    block_hi = ((iota((nq, LANES), 1) + 1) // BS + blk - 1) % blk
    spread_hi = (iota((nq, LANES), 0) == me * blk + block_hi).astype(F32).astype(BF16)
    row_lane_hi = dot(at_block8, spread_hi, ((1,), (0,)))[0:1]
    row_blk = dot(at_block8, pick, ((1,), (0,)))[0:1]
    be = (jnp.broadcast_to(row_lane, (count, LANES)) == iota((count, LANES), 0).astype(F32)).astype(F32)
    be3 = jnp.concatenate([be] * 3, axis=0).astype(BF16)
    be_hi = (jnp.broadcast_to(row_lane_hi, (count, LANES)) == iota((count, LANES), 0).astype(F32)).astype(F32)
    be3_hi = jnp.concatenate([be_hi] * 3, axis=0).astype(BF16)
    sel_tk = (jnp.broadcast_to(row_blk, (count, blk)) == iota((count, blk), 0).astype(F32)).astype(F32)


    linkf = jnp.concatenate([link[k, 0] for k in range(6)] + [jnp.zeros((2, blk), jnp.int32)], axis=0)
    over = (iota((blk, LANES), 0) == iota((blk, LANES), 1) // BS).astype(F32).astype(BF16)
    over_hi = (iota((blk, LANES), 0) == ((iota((blk, LANES), 1) + 1) // BS + blk - 1) % blk).astype(F32).astype(BF16)
    linkb = linkf.astype(F32).astype(BF16)
    mask = dot(linkb, over, ((1,), (0,)))
    mask_hi = dot(linkb, over_hi, ((1,), (0,)))
    is_lo = lane % BS == 0
    at_end = is_lo | (lane % BS == BS - 1)
    zmask = jnp.where(even, mask[4:5], mask_hi[5:6]) > 0.5
    half_lane = (iota((8, LANES), 1) % BS) // 2
    even8 = iota((8, LANES), 1) % 2 == 0
    pair8 = (((iota((8, LANES), 1) + 1) // 2) % 8) // 2

    def expand(level):
        for c in range(chunks):
            rows = stacked(srecv[level, pl.ds(c, count, stride=16), :])
            if c * LANES < 1600:
                xt[pl.ds(c * LANES, LANES), :] = dot(rows, be3, ((0,), (0,)))
            if (c + 1) * LANES > 1600:
                skip = max(0, 1600 - c * LANES)
                xt[pl.ds(c * LANES + skip, LANES - skip), :] = dot(rows, be3_hi, ((0,), (0,)))[skip:]
        for k in range(20):
            tile = xt[pl.ds(k * 64, 8, stride=8), :]
            for b in range(1, 8):
                tile = jnp.where(half_lane == b, xt[pl.ds(k * 64 + b, 8, stride=8), :], tile)
            cxy[pl.ds(k * BS, 8, stride=2), :] = tile
            cxy[pl.ds(k * BS + 1, 8, stride=2), :] = tile
        for k in range(10):
            tile = None
            for a in range(4):
                at = ((k // 2) * 8 + 4 * (k % 2) + a) * 8
                piece = jnp.where(even8, xt[pl.ds(1280 + at, 8), :], xt[pl.ds(1600 + at, 8), :])
                tile = piece if a == 0 else jnp.where(pair8 == a, piece, tile)
            cz[pl.ds(k * BS, 8, stride=2), :] = tile
            cz[pl.ds(k * BS + 1, 8, stride=2), :] = tile

    def across(u, pr, d, edge):
        axis = d - 1
        fc, sc = flux(u, pr, d)
        ub = [pltpu.roll(a, 1, axis) for a in u]
        fb = [ub[1 + d] if i == 0 else pltpu.roll(fc[i], 1, axis) for i in range(5)]
        low = interface(ub, fb, pltpu.roll(sc, 1, axis), u, fc, sc)
        low = [jnp.where(edge, 0.0, a) for a in low]
        return [pltpu.roll(a, a.shape[axis] - 1, axis) - a for a in low]

    is_lo8 = iota((8, LANES), 1) % BS == 0

    def inner(ref, dst):
        def along_xz(half):
            def tile(f, x):
                return ref[f, pl.ds(pl.multiple_of(x * BS + half, 8), 8), :]

            def step_x(x, hxl, u, pr, last):
                if last:
                    total = [-a for a in hxl]
                    hxr, un, prn = hxl, u, pr
                else:
                    un = [tile(f, x + 1) for f in range(5)]
                    prn = prim(un)
                    fc, sc = flux(u, pr, 0)
                    fn, sn = flux(un, prn, 0)
                    hxr = interface(u, fc, sc, un, fn, sn)
                    total = [hxr[f] - hxl[f] for f in range(5)]
                change = across(u, pr, 2, is_lo8)
                at = pl.multiple_of(x * BS + half, 8)
                for f in range(5):
                    dst[f, pl.ds(at, 8), :] = u[f] - (0.5 * LAMBDA) * (total[f] + change[f])
                return hxr, un, prn

            u = [tile(f, 0) for f in range(5)]
            zero = [jnp.zeros((8, LANES), F32)] * 5
            carry = lax.fori_loop(
                0, BS - 1, lambda x, carry: step_x(x, *carry, False), (zero, u, prim(u)), unroll=3
            )
            step_x(BS - 1, *carry, True)

        def along_y(x, carry):
            at = pl.ds(pl.multiple_of(x * BS, BS), BS)
            u = [ref[f, at, :] for f in range(5)]
            change = across(u, prim(u), 1, sub == 0)
            for f in range(5):
                dst[f, at, :] = dst[f, at, :] - (0.5 * LAMBDA) * change[f]
            return carry

        along_xz(0)
        along_xz(8)
        lax.fori_loop(0, BS, along_y, 0, unroll=2)

    def faces(ghost, cells, d, sign):
        gf, gs = flux(ghost, prim(ghost), d)
        cf, cs = flux(cells, prim(cells), d)
        return interface(ghost, gf, gs, cells, cf, cs, sign)

    def outer(ref, dst, step, after):
        for d in range(2):
            for side in range(2):
                chosen = jnp.broadcast_to(mask[2 * d + side:2 * d + side + 1], (BS, LANES)) > 0.5
                halo = hx if d == 0 else hy
                if d == 0:
                    rows = pl.ds(side * (BS - 1) * BS, BS)
                else:
                    rows = pl.ds(side * (BS - 1), BS, stride=BS)
                ghost = [
                    jnp.where(chosen, halo[step, side, f], cxy[pl.ds(((2 * d + side) * 5 + f) * BS, BS), :])
                    for f in range(5)
                ]
                cells = [ref[f, rows, :] for f in range(5)]
                face = faces(ghost, cells, d, 1.0 - 2 * side)
                for f in range(5):
                    dst[f, rows, :] = dst[f, rows, :] + (0.5 - side) * LAMBDA * face[f]
        comb = []
        for k in range(2):
            left = pltpu.roll(hz[step, 0, k], 1, 1)
            right = pltpu.roll(hz[step, 1, k], LANES - 1, 1)
            comb.append(jnp.where(even, left, right))
        sign = jnp.where(even, 1.0, -1.0)
        scale = (0.5 * LAMBDA) * sign
        for g in range(2):
            cells, ghost = [], []
            for f in range(5):
                k = f * 2 + g
                tile = cells_z[k]
                near = jnp.where(even, pltpu.roll(tile, 1, 1), pltpu.roll(tile, LANES - 1, 1))
                far = comb[k // 8]
                if k % 8:
                    far = pltpu.roll(far, LANES - 16 * (k % 8), 1)
                fine_side = jnp.where(first_pairs, far, near)
                cells.append(tile)
                ghost.append(jnp.where(zmask, fine_side, cz[pl.ds(k * BS, BS), :]))
            face = faces(ghost, cells, 2, sign)
            for f in range(5):
                change = scale * face[f]
                for x in range(8):
                    moved = change if x == 0 else pltpu.roll(change, LANES - 2 * x, 1)
                    rows = pl.ds((8 * g + x) * BS, BS)
                    dst[f, rows, :] = dst[f, rows, :] + jnp.where(at_end, moved, 0.0)
            after(g)

    inner(s0, s1)
    stage_level(1)
    mid_copies = exchange(1, sstage.at[1], srecv.at[1], 32)
    for copy in now_copies:
        copy.wait_recv()
    expand(0)
    for copy in halo0:
        copy.wait()
    outer(s0, s1, 0, lambda g: None)
    halo1 = halos(s1, 1)
    inner(s1, out)
    for copy in mid_copies:
        copy.wait_recv()
    expand(1)
    for copy in halo1:
        copy.wait()
    interleave = (iota((LANES, 8 * LANES), 0) == iota((LANES, 8 * LANES), 1) // 8).astype(F32).astype(BF16)
    lane8 = iota((blk, LANES), 1) % 8
    used = 5 * 64
    sel_rows = beside(sel_tk, blk)

    def means(g):
        for f in range(5):
            for a in range(4):
                total = None
                for x in range(2):
                    for y in range(2):
                        piece = out[f, pl.ds((8 * g + 2 * a + x) * BS + y, 8, stride=2), :]
                        total = piece if total is None else total + piece
                xy[pl.ds(g * 160 + f * 32 + a * 8, 8), :] = 0.125 * total

    def rows_out(c):
        size = min(LANES, used - c * LANES)
        block = xy[pl.ds(c * LANES, LANES), :]
        if size < LANES:
            block = jnp.where(iota((LANES, LANES), 0) < size, block, 0.0)
        zt[...] = block.T
        rows = jnp.concatenate(
            [zt[pl.ds(2 * z, blk, stride=BS), :] + zt[pl.ds(2 * z + 1, blk, stride=BS), :] for z in range(8)],
            axis=0,
        )
        wide = dot(jnp.concatenate(parts_of(rows, 3), axis=0).astype(BF16), interleave, ((1,), (0,)))
        wide = wide[:64] + wide[64:128] + wide[128:]
        tiles = []
        for g in range(size // 16):
            tile = wide[0:8, g * LANES:(g + 1) * LANES]
            for z in range(1, 8):
                tile = jnp.where(lane8 == z, wide[z * 8:z * 8 + 8, g * LANES:(g + 1) * LANES], tile)
            tiles.append(tile)
        routed = dot(sel_rows, stacked(jnp.concatenate(tiles, axis=1)), ((1,), (0,)))
        stage, first, each = (rstage, 0, 8) if c == 0 else (rstage2, (c - 1) * 8, rchunks - 8)
        for g in range(size // 16):
            stage[pl.ds(first + g, count, stride=each), :] = routed[:, g * LANES:(g + 1) * LANES]

    back = []

    def after(g):
        means(g)
        if g == 0:
            rows_out(0)
            back.append(exchange(2, rstage, rrecv, 2 * 8))
        else:
            rows_out(1)
            rows_out(2)
            back.append(exchange(3, rstage2, rrecv2, 2 * (rchunks - 8)))

    outer(s1, out, 1, after)
    sel = beside(sel_st, count)
    for half, (recv, first, each) in enumerate(((rrecv, 0, 8), (rrecv2, 8, rchunks - 8))):
        for copy in back[half]:
            copy.wait_recv()
        for c in range(each):
            rows = recv[pl.ds(c, count, stride=each), :]
            start = (first + c) * 16
            g, f, pairs = start // 160, start % 160 // 32, start % 32 // 16
            coarse[0, :, pl.ds((f * 4 + 2 * g + pairs) * LANES, LANES)] = dot(sel, stacked(rows), ((1,), (0,)))
    for copy in now_copies + mid_copies + back[0] + back[1]:
        copy.wait_send()


def place(out, coarse, out_new, coarse_new, sem):
    copies = [pltpu.make_async_copy(out.at[f], out_new.at[f], sem.at[f]) for f in range(5)]
    copies.append(pltpu.make_async_copy(coarse, coarse_new, sem.at[5]))
    for copy in copies:
        copy.start()
    for copy in copies:
        copy.wait()


def shards(n, fine, shell, parent, link):
    group = n[1] * n[2]
    count = 2 * group
    rwidth = 5 * (BS // 2) ** 3
    fine2 = fine.reshape(5, BS * BS, LANES)
    vmem = pl.BlockSpec(memory_space=pltpu.VMEM)
    out, coarse = pl.pallas_call(
        functools.partial(kernel, n),
        out_shape=(
            pltpu.VMEM((5, BS * BS, LANES), F32),
            pltpu.VMEM((1, shell.shape[1], rwidth), F32),
        ),
        in_specs=[pl.BlockSpec(memory_space=pltpu.HBM)] * 4,
        out_specs=(vmem, vmem),
        scratch_shapes=[
            pltpu.VMEM(shell.shape, F32),
            pltpu.VMEM(parent.shape, jnp.int32),
            pltpu.VMEM(link.shape, jnp.int32),
            pltpu.VMEM((5, BS * BS, LANES), F32),
            pltpu.VMEM((5, BS * BS, LANES), F32),
            pltpu.VMEM((2, 2, 5, BS, LANES), F32),
            pltpu.VMEM((2, 2, BS, LANES), F32),
            pltpu.VMEM((2, 2, 5, BS, LANES), F32),
            pltpu.VMEM((2, 2, 5, BS, LANES), F32),
            pltpu.VMEM((2, 2, 2, BS, LANES), F32),
            pltpu.VMEM((2, count * 16, LANES), F32),
            pltpu.VMEM((2, count * 16, LANES), F32),
            pltpu.VMEM((count * 8, LANES), F32),
            pltpu.VMEM((count * 8, LANES), F32),
            pltpu.VMEM((count * (rwidth // LANES - 8), LANES), F32),
            pltpu.VMEM((count * (rwidth // LANES - 8), LANES), F32),
            pltpu.VMEM((1920, LANES), F32),
            pltpu.VMEM((20 * BS, LANES), F32),
            pltpu.VMEM((10 * BS, LANES), F32),
            pltpu.VMEM((10, BS, LANES), F32),
            pltpu.VMEM((384, LANES), F32),
            pltpu.VMEM((LANES, LANES), F32),
            pltpu.SemaphoreType.DMA((8,)),
            pltpu.SemaphoreType.DMA((2, 6)),
            pltpu.SemaphoreType.DMA((2, 6)),
            pltpu.SemaphoreType.DMA((4, group)),
            pltpu.SemaphoreType.DMA((4, group)),
        ],
        compiler_params=pltpu.CompilerParams(
            collective_id=0, has_side_effects=True, vmem_limit_bytes=62 * 1024 * 1024
        ),
    )(fine2, shell, parent, link)
    hbm = pl.BlockSpec(memory_space=pltpu.HBM)
    out, coarse = pl.pallas_call(
        place,
        out_shape=(jax.ShapeDtypeStruct(out.shape, F32), jax.ShapeDtypeStruct(coarse.shape, F32)),
        in_specs=[vmem, vmem],
        out_specs=(hbm, hbm),
        scratch_shapes=[pltpu.SemaphoreType.DMA((6,))],
        compiler_params=pltpu.CompilerParams(vmem_limit_bytes=4 * 1024 * 1024),
    )(out, coarse)
    return out.reshape(fine.shape), coarse


def solution(mesh):
    n = (mesh.shape["gx"], mesh.shape["gy"], mesh.shape["gz"])
    return jax.shard_map(
        functools.partial(shards, n),
        mesh=mesh,
        in_specs=(
            P(None, "gx", "gy", "gz"),
            P("gx", ("gy", "gz"), None),
            P("gx", None),
            P(None, "gx", "gy", "gz"),
        ),
        out_specs=(P(None, "gx", "gy", "gz"), P("gx", ("gy", "gz"), None)),
        check_vma=False,
    )
```

```python
import functools

import jax
import jax.numpy as jnp
from jax import lax
from jax.experimental import pallas as pl
from jax.experimental.pallas import tpu as pltpu
from jax.sharding import PartitionSpec as P

BS = 16
GAMMA = 1.4
LAMBDA = 0.05
LANES = 128
MESH = pl.DeviceIdType.MESH
F32 = jnp.float32
BF16 = jnp.bfloat16


def iota(shape, dim):
    return lax.broadcasted_iota(jnp.int32, shape, dim)


def parts_of(x, count):
    result = []
    for _ in range(count - 1):
        head = x.astype(BF16).astype(F32)
        result.append(head)
        x = x - head
    result.append(x)
    return result


def dot(a, b, contract):
    return lax.dot_general(a, b, (contract, ((), ())), preferred_element_type=F32)


def stacked(x):
    pieces = parts_of(x, 3)
    if x.shape[0] % 16:
        pieces.append(jnp.zeros_like(x))
    return jnp.concatenate(pieces, axis=0).astype(BF16)


def beside(x, rows):
    count = 4 if rows % 16 else 3
    return jnp.concatenate([x] * count, axis=1).astype(BF16)


def prim(u):
    inv = 1.0 / u[0]
    vel = [u[1] * inv, u[2] * inv, u[3] * inv]
    press = (GAMMA - 1.0) * (u[4] - 0.5 * (u[1] * vel[0] + u[2] * vel[1] + u[3] * vel[2]))
    sound = jnp.sqrt(GAMMA * press * inv)
    return vel, press, sound


def flux(u, pr, d):
    vel, press, sound = pr
    vd = vel[d]
    f = [u[1 + d], u[1] * vd, u[2] * vd, u[3] * vd, (u[4] + press) * vd]
    f[1 + d] = f[1 + d] + press
    return f, jnp.abs(vd) + sound


def interface(ul, fl, sl, ur, fr, sr, sign=None):
    wave = jnp.maximum(sl, sr)
    if sign is not None:
        wave = sign * wave
    return [(fl[i] + fr[i]) - wave * (ur[i] - ul[i]) for i in range(5)]


def kernel(
    n,
    fine, shell_hbm, parent_hbm, link_hbm, out, coarse,
    shell, parent, link, s0, s1, ypack, zpack, hx, hy, hz, sstage, srecv, rstage, rrecv, rstage2, rrecv2, xt, cxy, cz, cells_z, xy, zt,
    load_sem, halo_send, halo_recv, all_send, all_recv,
):
    nx, ny, nz = n
    group = ny * nz
    count = 2 * group
    gx, gy, gz = lax.axis_index("gx"), lax.axis_index("gy"), lax.axis_index("gz")
    me = gy * nz + gz
    blk = shell.shape[1]
    width = shell.shape[2] // 2
    chunks = width // LANES
    rwidth = coarse.shape[2]
    rchunks = rwidth // LANES
    nq = parent.shape[1]
    peers = []
    order = sorted(range(1, group), key=lambda i: i % nz == 0)
    for i in order:
        peer = lax.rem(me + i, group)
        peers.append((gx, peer // nz, lax.rem(peer, nz)))
    xlo, xhi = (lax.rem(gx + nx - 1, nx), gy, gz), (lax.rem(gx + 1, nx), gy, gz)
    ylo, yhi = (gx, lax.rem(gy + ny - 1, ny), gz), (gx, lax.rem(gy + 1, ny), gz)
    zlo, zhi = (gx, gy, lax.rem(gz + nz - 1, nz)), (gx, gy, lax.rem(gz + 1, nz))

    barrier = pltpu.get_barrier_semaphore()
    greeted = peers + [xlo, xhi]
    for dev in greeted:
        pl.semaphore_signal(barrier, inc=1, device_id=dev, device_id_type=MESH)

    loads = []
    for k, (src, dst) in enumerate(((parent_hbm, parent), (shell_hbm, shell), (link_hbm, link))):
        load = pltpu.make_async_copy(src, dst, load_sem.at[5 + k])
        load.start()
        loads.append(load)
    for f in range(5):
        load = pltpu.make_async_copy(fine.at[f], s0.at[f], load_sem.at[f])
        load.start()
        loads.append(load)

    loads[0].wait()
    par = parent[...]
    lane_q = iota((1, nq), 1)
    owner = par // blk
    rank = jnp.zeros((1, nq), jnp.int32)
    for j in range(1, blk):
        before = pltpu.roll(jnp.broadcast_to(owner, (8, nq)), j, 1)[0:1]
        rank = rank + jnp.where((lane_q % blk >= j) & (before == owner), 1, 0)
    at_owner = (lane_q // blk) * 2 + rank
    at_block = owner * 2 + rank
    to_t = (jnp.broadcast_to(at_owner, (count, nq)) == iota((count, nq), 0)).astype(F32).astype(BF16)
    mine = (jnp.broadcast_to(par, (blk, nq)) == me * blk + iota((blk, nq), 0)).astype(F32).astype(BF16)
    sel_ts = dot(to_t, mine, ((1,), (1,)))

    loads[1].wait()
    sel = beside(sel_ts, blk)

    def stage_level(level):
        for c in range(chunks):
            value = shell[0, :, pl.ds(c * LANES, LANES)]
            if level:
                value = 0.5 * (value + shell[0, :, pl.ds(width + c * LANES, LANES)])
            sstage[level, pl.ds(c, count, stride=16), :] = dot(sel, stacked(value), ((1,), (0,)))

    stage_level(0)

    lane = iota((BS, LANES), 1)
    sub = iota((BS, LANES), 0)
    even = lane % 2 == 0
    pair = ((lane + 1) // 2) % 8
    first_pairs = (lane + 1) % LANES < 16

    def plane(ref, f, x):
        return ref[f, pl.ds(x * BS, BS), :]

    def pack_y(ref, step):
        for f in range(5):
            ypack[step, 0, f] = ref[f, pl.ds(0, BS, stride=BS), :]
            ypack[step, 1, f] = ref[f, pl.ds(BS - 1, BS, stride=BS), :]

    def pack_z(ref, step):
        packed = [jnp.zeros((BS, LANES), F32)] * 2
        for f in range(5):
            for g in range(2):
                tile = plane(ref, f, 8 * g)
                for x in range(1, 8):
                    tile = jnp.where(pair == x, pltpu.roll(plane(ref, f, 8 * g + x), 2 * x, 1), tile)
                k = f * 2 + g
                cells_z[k] = tile
                moved = tile if k % 8 == 0 else pltpu.roll(tile, 16 * (k % 8), 1)
                packed[k // 8] = jnp.where(((lane + 1) // 16) % 8 == k % 8, moved, packed[k // 8])
        zpack[step, 0] = packed[0]
        zpack[step, 1] = packed[1]

    def halos(ref, step):
        copies = []

        def send(k, src, dst, dev):
            copy = pltpu.make_async_remote_copy(
                src_ref=src, dst_ref=dst, send_sem=halo_send.at[step, k], recv_sem=halo_recv.at[step, k],
                device_id=dev, device_id_type=MESH,
            )
            copy.start()
            copies.append(copy)

        send(0, ref.at[:, pl.ds(BS * BS - BS, BS)], hx.at[step, 0], xhi)
        send(1, ref.at[:, pl.ds(0, BS)], hx.at[step, 1], xlo)
        pack_z(ref, step)
        send(4, zpack.at[step], hz.at[step, 0], zhi)
        send(5, zpack.at[step], hz.at[step, 1], zlo)
        pack_y(ref, step)
        send(2, ypack.at[step, 1], hy.at[step, 0], yhi)
        send(3, ypack.at[step, 0], hy.at[step, 1], ylo)
        return copies

    def exchange(kind, stage, recv, rows):
        copies = []
        for i, dev in zip(order, peers):
            to = lax.rem(me + i, group)
            copy = pltpu.make_async_remote_copy(
                src_ref=stage.at[pl.ds(pl.multiple_of(to * rows, 8), rows)],
                dst_ref=recv.at[pl.ds(pl.multiple_of(me * rows, 8), rows)],
                send_sem=all_send.at[kind, i], recv_sem=all_recv.at[kind, i],
                device_id=dev, device_id_type=MESH,
            )
            copy.start()
            copies.append(copy)
        own = pl.ds(pl.multiple_of(me * rows, 8), rows)
        recv[own, :] = stage[own, :]
        return copies

    for load in loads[2:]:
        load.wait()
    pl.semaphore_wait(barrier, len(greeted))
    now_copies = exchange(0, sstage.at[0], srecv.at[0], 32)
    halo0 = halos(s0, 0)

    sel_st = dot(mine, to_t, ((1,), (1,)))
    at_block8 = jnp.broadcast_to(at_block.astype(F32), (8, nq)).astype(BF16)
    spread = (iota((nq, LANES), 0) == me * blk + iota((nq, LANES), 1) // BS).astype(F32).astype(BF16)
    pick = (iota((nq, blk), 0) == me * blk + iota((nq, blk), 1)).astype(F32).astype(BF16)
    row_lane = dot(at_block8, spread, ((1,), (0,)))[0:1]
    block_hi = ((iota((nq, LANES), 1) + 1) // BS + blk - 1) % blk
    spread_hi = (iota((nq, LANES), 0) == me * blk + block_hi).astype(F32).astype(BF16)
    row_lane_hi = dot(at_block8, spread_hi, ((1,), (0,)))[0:1]
    row_blk = dot(at_block8, pick, ((1,), (0,)))[0:1]
    be = (jnp.broadcast_to(row_lane, (count, LANES)) == iota((count, LANES), 0).astype(F32)).astype(F32)
    be3 = jnp.concatenate([be] * 3, axis=0).astype(BF16)
    be_hi = (jnp.broadcast_to(row_lane_hi, (count, LANES)) == iota((count, LANES), 0).astype(F32)).astype(F32)
    be3_hi = jnp.concatenate([be_hi] * 3, axis=0).astype(BF16)
    sel_tk = (jnp.broadcast_to(row_blk, (count, blk)) == iota((count, blk), 0).astype(F32)).astype(F32)


    linkf = jnp.concatenate([link[k, 0] for k in range(6)] + [jnp.zeros((2, blk), jnp.int32)], axis=0)
    over = (iota((blk, LANES), 0) == iota((blk, LANES), 1) // BS).astype(F32).astype(BF16)
    over_hi = (iota((blk, LANES), 0) == ((iota((blk, LANES), 1) + 1) // BS + blk - 1) % blk).astype(F32).astype(BF16)
    linkb = linkf.astype(F32).astype(BF16)
    mask = dot(linkb, over, ((1,), (0,)))
    mask_hi = dot(linkb, over_hi, ((1,), (0,)))
    is_lo = lane % BS == 0
    at_end = is_lo | (lane % BS == BS - 1)
    zmask = jnp.where(even, mask[4:5], mask_hi[5:6]) > 0.5
    half_lane = (iota((8, LANES), 1) % BS) // 2
    even8 = iota((8, LANES), 1) % 2 == 0
    pair8 = (((iota((8, LANES), 1) + 1) // 2) % 8) // 2

    def expand(level):
        for c in range(chunks):
            rows = stacked(srecv[level, pl.ds(c, count, stride=16), :])
            if c * LANES < 1600:
                xt[pl.ds(c * LANES, LANES), :] = dot(rows, be3, ((0,), (0,)))
            if (c + 1) * LANES > 1600:
                skip = max(0, 1600 - c * LANES)
                xt[pl.ds(c * LANES + skip, LANES - skip), :] = dot(rows, be3_hi, ((0,), (0,)))[skip:]
        for k in range(20):
            tile = xt[pl.ds(k * 64, 8, stride=8), :]
            for b in range(1, 8):
                tile = jnp.where(half_lane == b, xt[pl.ds(k * 64 + b, 8, stride=8), :], tile)
            cxy[pl.ds(k * BS, 8, stride=2), :] = tile
            cxy[pl.ds(k * BS + 1, 8, stride=2), :] = tile
        for k in range(10):
            tile = None
            for a in range(4):
                at = ((k // 2) * 8 + 4 * (k % 2) + a) * 8
                piece = jnp.where(even8, xt[pl.ds(1280 + at, 8), :], xt[pl.ds(1600 + at, 8), :])
                tile = piece if a == 0 else jnp.where(pair8 == a, piece, tile)
            cz[pl.ds(k * BS, 8, stride=2), :] = tile
            cz[pl.ds(k * BS + 1, 8, stride=2), :] = tile

    def across(u, pr, d, edge):
        axis = d - 1
        fc, sc = flux(u, pr, d)
        ub = [pltpu.roll(a, 1, axis) for a in u]
        fb = [ub[1 + d] if i == 0 else pltpu.roll(fc[i], 1, axis) for i in range(5)]
        low = interface(ub, fb, pltpu.roll(sc, 1, axis), u, fc, sc)
        low = [jnp.where(edge, 0.0, a) for a in low]
        return [pltpu.roll(a, a.shape[axis] - 1, axis) - a for a in low]

    is_lo8 = iota((8, LANES), 1) % BS == 0

    def inner(ref, dst):
        def along_xz(half):
            def tile(f, x):
                return ref[f, pl.ds(pl.multiple_of(x * BS + half, 8), 8), :]

            def step_x(x, hxl, u, pr, last):
                if last:
                    total = [-a for a in hxl]
                    hxr, un, prn = hxl, u, pr
                else:
                    un = [tile(f, x + 1) for f in range(5)]
                    prn = prim(un)
                    fc, sc = flux(u, pr, 0)
                    fn, sn = flux(un, prn, 0)
                    hxr = interface(u, fc, sc, un, fn, sn)
                    total = [hxr[f] - hxl[f] for f in range(5)]
                change = across(u, pr, 2, is_lo8)
                at = pl.multiple_of(x * BS + half, 8)
                for f in range(5):
                    dst[f, pl.ds(at, 8), :] = u[f] - (0.5 * LAMBDA) * (total[f] + change[f])
                return hxr, un, prn

            u = [tile(f, 0) for f in range(5)]
            zero = [jnp.zeros((8, LANES), F32)] * 5
            carry = lax.fori_loop(
                0, BS - 1, lambda x, carry: step_x(x, *carry, False), (zero, u, prim(u)), unroll=5
            )
            step_x(BS - 1, *carry, True)

        def along_y(x, carry):
            at = pl.ds(pl.multiple_of(x * BS, BS), BS)
            u = [ref[f, at, :] for f in range(5)]
            change = across(u, prim(u), 1, sub == 0)
            for f in range(5):
                dst[f, at, :] = dst[f, at, :] - (0.5 * LAMBDA) * change[f]
            return carry

        along_xz(0)
        along_xz(8)
        lax.fori_loop(0, BS, along_y, 0, unroll=4)

    def faces(ghost, cells, d, sign):
        gf, gs = flux(ghost, prim(ghost), d)
        cf, cs = flux(cells, prim(cells), d)
        return interface(ghost, gf, gs, cells, cf, cs, sign)

    def outer(ref, dst, step, after):
        for d in range(2):
            for side in range(2):
                chosen = jnp.broadcast_to(mask[2 * d + side:2 * d + side + 1], (BS, LANES)) > 0.5
                halo = hx if d == 0 else hy
                if d == 0:
                    rows = pl.ds(side * (BS - 1) * BS, BS)
                else:
                    rows = pl.ds(side * (BS - 1), BS, stride=BS)
                ghost = [
                    jnp.where(chosen, halo[step, side, f], cxy[pl.ds(((2 * d + side) * 5 + f) * BS, BS), :])
                    for f in range(5)
                ]
                cells = [ref[f, rows, :] for f in range(5)]
                face = faces(ghost, cells, d, 1.0 - 2 * side)
                for f in range(5):
                    dst[f, rows, :] = dst[f, rows, :] + (0.5 - side) * LAMBDA * face[f]
        comb = []
        for k in range(2):
            left = pltpu.roll(hz[step, 0, k], 1, 1)
            right = pltpu.roll(hz[step, 1, k], LANES - 1, 1)
            comb.append(jnp.where(even, left, right))
        sign = jnp.where(even, 1.0, -1.0)
        scale = (0.5 * LAMBDA) * sign
        for g in range(2):
            cells, ghost = [], []
            for f in range(5):
                k = f * 2 + g
                tile = cells_z[k]
                near = jnp.where(even, pltpu.roll(tile, 1, 1), pltpu.roll(tile, LANES - 1, 1))
                far = comb[k // 8]
                if k % 8:
                    far = pltpu.roll(far, LANES - 16 * (k % 8), 1)
                fine_side = jnp.where(first_pairs, far, near)
                cells.append(tile)
                ghost.append(jnp.where(zmask, fine_side, cz[pl.ds(k * BS, BS), :]))
            face = faces(ghost, cells, 2, sign)
            for f in range(5):
                change = scale * face[f]
                for x in range(8):
                    moved = change if x == 0 else pltpu.roll(change, LANES - 2 * x, 1)
                    rows = pl.ds((8 * g + x) * BS, BS)
                    dst[f, rows, :] = dst[f, rows, :] + jnp.where(at_end, moved, 0.0)
            after(g)

    inner(s0, s1)
    stage_level(1)
    mid_copies = exchange(1, sstage.at[1], srecv.at[1], 32)
    for copy in now_copies:
        copy.wait_recv()
    expand(0)
    for copy in halo0:
        copy.wait()
    outer(s0, s1, 0, lambda g: None)
    halo1 = halos(s1, 1)
    inner(s1, out)
    for copy in mid_copies:
        copy.wait_recv()
    expand(1)
    for copy in halo1:
        copy.wait()
    interleave = (iota((LANES, 8 * LANES), 0) == iota((LANES, 8 * LANES), 1) // 8).astype(F32).astype(BF16)
    lane8 = iota((blk, LANES), 1) % 8
    used = 5 * 64
    sel_rows = beside(sel_tk, blk)

    def means(g):
        for f in range(5):
            for a in range(4):
                total = None
                for x in range(2):
                    for y in range(2):
                        piece = out[f, pl.ds((8 * g + 2 * a + x) * BS + y, 8, stride=2), :]
                        total = piece if total is None else total + piece
                xy[pl.ds(g * 160 + f * 32 + a * 8, 8), :] = 0.125 * total

    def rows_out(c):
        size = min(LANES, used - c * LANES)
        block = xy[pl.ds(c * LANES, LANES), :]
        if size < LANES:
            block = jnp.where(iota((LANES, LANES), 0) < size, block, 0.0)
        zt[...] = block.T
        rows = jnp.concatenate(
            [zt[pl.ds(2 * z, blk, stride=BS), :] + zt[pl.ds(2 * z + 1, blk, stride=BS), :] for z in range(8)],
            axis=0,
        )
        wide = dot(jnp.concatenate(parts_of(rows, 3), axis=0).astype(BF16), interleave, ((1,), (0,)))
        wide = wide[:64] + wide[64:128] + wide[128:]
        tiles = []
        for g in range(size // 16):
            tile = wide[0:8, g * LANES:(g + 1) * LANES]
            for z in range(1, 8):
                tile = jnp.where(lane8 == z, wide[z * 8:z * 8 + 8, g * LANES:(g + 1) * LANES], tile)
            tiles.append(tile)
        routed = dot(sel_rows, stacked(jnp.concatenate(tiles, axis=1)), ((1,), (0,)))
        stage, first, each = (rstage, 0, 8) if c == 0 else (rstage2, (c - 1) * 8, rchunks - 8)
        for g in range(size // 16):
            stage[pl.ds(first + g, count, stride=each), :] = routed[:, g * LANES:(g + 1) * LANES]

    back = []

    def after(g):
        means(g)
        if g == 0:
            rows_out(0)
            back.append(exchange(2, rstage, rrecv, 2 * 8))
        else:
            rows_out(1)
            rows_out(2)
            back.append(exchange(3, rstage2, rrecv2, 2 * (rchunks - 8)))

    outer(s1, out, 1, after)
    sel = beside(sel_st, count)
    for half, (recv, first, each) in enumerate(((rrecv, 0, 8), (rrecv2, 8, rchunks - 8))):
        for copy in back[half]:
            copy.wait_recv()
        for c in range(each):
            rows = recv[pl.ds(c, count, stride=each), :]
            start = (first + c) * 16
            g, f, pairs = start // 160, start % 160 // 32, start % 32 // 16
            coarse[0, :, pl.ds((f * 4 + 2 * g + pairs) * LANES, LANES)] = dot(sel, stacked(rows), ((1,), (0,)))
    for copy in now_copies + mid_copies + back[0] + back[1]:
        copy.wait_send()


def place(out, coarse, out_new, coarse_new, sem):
    copies = [pltpu.make_async_copy(out.at[f], out_new.at[f], sem.at[f]) for f in range(5)]
    copies.append(pltpu.make_async_copy(coarse, coarse_new, sem.at[5]))
    for copy in copies:
        copy.start()
    for copy in copies:
        copy.wait()


def shards(n, fine, shell, parent, link):
    group = n[1] * n[2]
    count = 2 * group
    rwidth = 5 * (BS // 2) ** 3
    fine2 = fine.reshape(5, BS * BS, LANES)
    vmem = pl.BlockSpec(memory_space=pltpu.VMEM)
    out, coarse = pl.pallas_call(
        functools.partial(kernel, n),
        out_shape=(
            pltpu.VMEM((5, BS * BS, LANES), F32),
            pltpu.VMEM((1, shell.shape[1], rwidth), F32),
        ),
        in_specs=[pl.BlockSpec(memory_space=pltpu.HBM)] * 4,
        out_specs=(vmem, vmem),
        scratch_shapes=[
            pltpu.VMEM(shell.shape, F32),
            pltpu.VMEM(parent.shape, jnp.int32),
            pltpu.VMEM(link.shape, jnp.int32),
            pltpu.VMEM((5, BS * BS, LANES), F32),
            pltpu.VMEM((5, BS * BS, LANES), F32),
            pltpu.VMEM((2, 2, 5, BS, LANES), F32),
            pltpu.VMEM((2, 2, BS, LANES), F32),
            pltpu.VMEM((2, 2, 5, BS, LANES), F32),
            pltpu.VMEM((2, 2, 5, BS, LANES), F32),
            pltpu.VMEM((2, 2, 2, BS, LANES), F32),
            pltpu.VMEM((2, count * 16, LANES), F32),
            pltpu.VMEM((2, count * 16, LANES), F32),
            pltpu.VMEM((count * 8, LANES), F32),
            pltpu.VMEM((count * 8, LANES), F32),
            pltpu.VMEM((count * (rwidth // LANES - 8), LANES), F32),
            pltpu.VMEM((count * (rwidth // LANES - 8), LANES), F32),
            pltpu.VMEM((1920, LANES), F32),
            pltpu.VMEM((20 * BS, LANES), F32),
            pltpu.VMEM((10 * BS, LANES), F32),
            pltpu.VMEM((10, BS, LANES), F32),
            pltpu.VMEM((384, LANES), F32),
            pltpu.VMEM((LANES, LANES), F32),
            pltpu.SemaphoreType.DMA((8,)),
            pltpu.SemaphoreType.DMA((2, 6)),
            pltpu.SemaphoreType.DMA((2, 6)),
            pltpu.SemaphoreType.DMA((4, group)),
            pltpu.SemaphoreType.DMA((4, group)),
        ],
        compiler_params=pltpu.CompilerParams(
            collective_id=0, has_side_effects=True, vmem_limit_bytes=62 * 1024 * 1024
        ),
    )(fine2, shell, parent, link)
    hbm = pl.BlockSpec(memory_space=pltpu.HBM)
    out, coarse = pl.pallas_call(
        place,
        out_shape=(jax.ShapeDtypeStruct(out.shape, F32), jax.ShapeDtypeStruct(coarse.shape, F32)),
        in_specs=[vmem, vmem],
        out_specs=(hbm, hbm),
        scratch_shapes=[pltpu.SemaphoreType.DMA((6,))],
        compiler_params=pltpu.CompilerParams(vmem_limit_bytes=4 * 1024 * 1024),
    )(out, coarse)
    return out.reshape(fine.shape), coarse


def solution(mesh):
    n = (mesh.shape["gx"], mesh.shape["gy"], mesh.shape["gz"])
    return jax.shard_map(
        functools.partial(shards, n),
        mesh=mesh,
        in_specs=(
            P(None, "gx", "gy", "gz"),
            P("gx", ("gy", "gz"), None),
            P("gx", None),
            P(None, "gx", "gy", "gz"),
        ),
        out_specs=(P(None, "gx", "gy", "gz"), P("gx", ("gy", "gz"), None)),
        check_vma=False,
    )
```
